256 devices in a mesh: batch: 32 (over x, z_lo, core), field: 8 (over z_hi, y).
Axes of the slice: x: 4, y: 4, z: 8 (z_hi: 2, z_lo: 4; z = z_hi * 4 + z_lo), core: 2. Of those that a mesh axis runs over, the one named last changes fastest.
Arguments:
- embeddings: bfloat16 [4096, 768, 192], P('batch', 'field'), may hold values from -6 to 6
- compress: bfloat16 [768, 16], P('field'), may hold values from -0.21875 to 0.21875
- w_up: bfloat16 [1024, 12288], P(None, 'field'), may hold values from -0.0546875 to 0.0546875
- up_bias: float32 [1024], replicated, may hold values from -3 to 3
- w_down: bfloat16 [1024, 9216], P(None, 'field'), may hold values from -0.1875 to 0.1875
- w_linear: bfloat16 [768, 96], P('field'), may hold values from -0.21875 to 0.21875
- ln_gain: float32 [192], replicated, may hold values from 0.5 to 1.5
- cot_fm: bfloat16 [4096, 48, 192], P('batch', 'field'), may hold values from -0.09375 to 0.09375
- cot_lc: bfloat16 [4096, 96, 192], P('batch', 'field'), may hold values from -0.09375 to 0.09375
Outputs:
- fm_out: bfloat16 [4096, 48, 192], P('batch', 'field')
- lc_out: bfloat16 [4096, 96, 192], P('batch', 'field')
- grad_compress: float32 [768, 16], P('field')
- grad_up: float32 [1024, 12288], P('batch', 'field')
- grad_bias: float32 [1024], replicated
- grad_down: float32 [1024, 9216], P('batch', 'field')
- grad_linear: float32 [768, 96], P('field')
- grad_gain: float32 [192], replicated
The draws below stay inside these ranges and needn't reach their ends.
All inputs are finite; a program needn't handle non-finite values.
Results may differ from the reference program's by a relative error of at most 0.012.
Values may be sent and summed in bfloat16 or wider, within the bound.
A program may use at most 128 MiB of HBM per device.

```python
import jax
import jax.numpy as jnp
from jax import lax

B_DEV = 128
F = 768
E = 192
K = 16
H = 1024
NF = 48
NL = 96
BATCH = 4096
N_BATCH = 32


def steps_of(rng, dims, cuts, smallest, largest):
    loudness, own = 1.0, jax.random.fold_in(rng, 6)
    for position, shards_of in cuts:
        steps = jnp.exp(jax.random.uniform(jax.random.fold_in(own, position), (shards_of,), jnp.float32, smallest / len(cuts), largest / len(cuts)))
        loudness = loudness * jnp.repeat(steps, dims[position] // shards_of).reshape([-1 if axis == position else 1 for axis in range(len(dims))])
    return loudness


def gaussian(stream_key, shape, spread, bound, split=(), dtype=jnp.bfloat16):
    values = spread * jax.random.normal(stream_key, shape, jnp.float32)
    if split:
        values = values * steps_of(stream_key, shape, split, -0.22, 0.18)
    return jnp.clip(values, -bound, bound).astype(dtype)


def setup_inputs(seed: int = 0) -> dict:
    keys = jax.random.split(jax.random.key(seed), 10)
    return {
        "embeddings": gaussian(keys[0], (BATCH, F, E), 1.0, 6.0, ((0, 32), (1, 8))),
        "compress": gaussian(keys[1], (F, K), F ** -0.5, 0.21875, ((0, 8),)),
        "w_up": gaussian(keys[2], (H, F * K), (F * K) ** -0.5, 0.0546875, ((1, 8),)),
        "up_bias": gaussian(keys[3], (H,), 0.5, 3.0, (), jnp.float32),
        "w_down": gaussian(keys[4], (H, NF * E), H ** -0.5, 0.1875, ((1, 8),)),
        "w_linear": gaussian(keys[5], (F, NL), F ** -0.5, 0.21875, ((0, 8),)),
        "ln_gain": jnp.clip(1.0 + 0.1 * jax.random.normal(keys[6], (E,), jnp.float32), 0.5, 1.5),
        "cot_fm": gaussian(keys[7], (BATCH, NF, E), (1.0 / (B_DEV * N_BATCH) ** 0.5), 0.09375, ((0, 32), (1, 8))),
        "cot_lc": gaussian(keys[8], (BATCH, NL, E), (1.0 / (B_DEV * N_BATCH) ** 0.5), 0.09375, ((0, 32), (1, 8))),
    }


def norm_rows(values):
    centre = values - lax.optimization_barrier(jnp.mean(values, axis=-1, keepdims=True))
    rstd = lax.rsqrt(lax.optimization_barrier(jnp.mean(centre * centre, axis=-1, keepdims=True)) + 1e-05)
    return (centre * rstd, rstd)

def norm_back(cotangent, normed, rstd, ln_gain):
    dn = cotangent * ln_gain
    return rstd * (dn - lax.optimization_barrier(jnp.mean(dn, axis=-1, keepdims=True)) - normed * lax.optimization_barrier(jnp.mean(dn * normed, axis=-1, keepdims=True)))

def reference(embeddings, compress, w_up, up_bias, w_down, w_linear, ln_gain, cot_fm, cot_lc):
    inv_root = jnp.float32(E) ** (-0.5)
    blocks = BATCH // B_DEV
    emb_blocks = embeddings.reshape(blocks, B_DEV, F, E)
    fm_blocks = cot_fm.reshape(blocks, B_DEV, NF, E)
    lc_blocks = cot_lc.reshape(blocks, B_DEV, NL, E)
    comp32 = compress.astype(jnp.float32)
    lin32 = w_linear.astype(jnp.float32)

    def block_step(totals, block):
        emb_block, cot_one, cot_two = block
        inputs = emb_block.astype(jnp.float32)
        compressed = jnp.einsum('bfe,fk->bke', inputs, comp32).astype(jnp.bfloat16)
        interact = (jnp.einsum('bfe,bke->bfk', inputs, compressed.astype(jnp.float32)) * inv_root).astype(jnp.bfloat16)
        flat = interact.reshape(B_DEV, F * K)
        hidden_pre = jnp.dot(flat, w_up.T, preferred_element_type=jnp.float32) + up_bias
        hidden = jax.nn.silu(hidden_pre).astype(jnp.bfloat16)
        fm_raw = jnp.dot(hidden, w_down, preferred_element_type=jnp.float32).reshape(B_DEV, NF, E)
        lc_raw = jnp.einsum('bfe,fn->bne', inputs, lin32)
        fm_normed, fm_rstd = norm_rows(fm_raw)
        lc_normed, lc_rstd = norm_rows(lc_raw)
        fm_out = (fm_normed * ln_gain).astype(jnp.bfloat16)
        lc_out = (lc_normed * ln_gain).astype(jnp.bfloat16)
        cot_a = cot_one.astype(jnp.float32)
        cot_b = cot_two.astype(jnp.float32)
        gain_part = lax.optimization_barrier(jnp.sum(cot_a * fm_normed, axis=(0, 1))) + lax.optimization_barrier(jnp.sum(cot_b * lc_normed, axis=(0, 1)))
        grad_fm = norm_back(cot_a, fm_normed, fm_rstd, ln_gain).astype(jnp.bfloat16).reshape(B_DEV, NF * E)
        grad_lc = norm_back(cot_b, lc_normed, lc_rstd, ln_gain).astype(jnp.bfloat16)
        down_part = jnp.dot(hidden.T, grad_fm, preferred_element_type=jnp.float32)
        grad_hidden = jnp.dot(grad_fm, w_down.T, preferred_element_type=jnp.float32)
        sigma = jax.nn.sigmoid(hidden_pre)
        grad_pre32 = grad_hidden * sigma * (1.0 + hidden_pre * (1.0 - sigma))
        bias_part = lax.optimization_barrier(jnp.sum(grad_pre32, axis=0))
        grad_pre = grad_pre32.astype(jnp.bfloat16)
        up_part = jnp.dot(grad_pre.T, flat, preferred_element_type=jnp.float32)
        grad_inter = jnp.dot(grad_pre, w_up, preferred_element_type=jnp.float32).astype(jnp.bfloat16).reshape(B_DEV, F, K)
        grad_comp = (jnp.einsum('bfk,bfe->bke', grad_inter.astype(jnp.float32), inputs) * inv_root).astype(jnp.bfloat16)
        comp_part = jnp.einsum('bfe,bke->fk', inputs, grad_comp.astype(jnp.float32))
        lin_part = jnp.einsum('bfe,bne->fn', inputs, grad_lc.astype(jnp.float32))
        sums = (totals[0] + comp_part, totals[1] + up_part, totals[2] + bias_part, totals[3] + down_part, totals[4] + lin_part, totals[5] + gain_part)
        return (sums, (fm_out, lc_out))
    start_totals = (jnp.zeros((F, K), jnp.float32), jnp.zeros((H, F * K), jnp.float32), jnp.zeros((H,), jnp.float32), jnp.zeros((H, NF * E), jnp.float32), jnp.zeros((F, NL), jnp.float32), jnp.zeros((E,), jnp.float32))
    totals, outputs = lax.scan(block_step, start_totals, (emb_blocks, fm_blocks, lc_blocks))
    fm_out = outputs[0].reshape(BATCH, NF, E)
    lc_out = outputs[1].reshape(BATCH, NL, E)
    return (fm_out, lc_out, totals[0], totals[1], totals[2], totals[3], totals[4], totals[5])
```

```python
import functools

import jax
import jax.numpy as jnp
from jax import lax
from jax.experimental import pallas as pl
from jax.experimental.pallas import tpu as pltpu
from jax.sharding import PartitionSpec as P

MESH = pl.DeviceIdType.MESH
VMEM = pltpu.VMEM
F32 = jnp.float32
BF16 = jnp.bfloat16
LIMIT = 48 * 1024 * 1024


class Place:
    def __init__(self):
        batch, field = lax.axis_index("batch"), lax.axis_index("field")
        self.batch, self.field = batch, field
        self.y, self.zh = lax.rem(field, 4), lax.div(field, 4)
        self.core = lax.rem(batch, 2)
        self.zl = lax.rem(lax.div(batch, 2), 4)
        self.x = lax.div(batch, 8)

    def to_y(self, k):
        other = lax.rem(self.y + k, 4)
        return other, (self.batch, self.zh * 4 + other)

    def to_zh(self):
        other = 1 - self.zh
        return other, (self.batch, other * 4 + self.y)

    def to_core(self):
        other = 1 - self.core
        return other, (self.x * 8 + self.zl * 2 + other, self.field)

    def to_x(self, k):
        other = lax.rem(self.x + k, 4)
        return other, (other * 8 + self.zl * 2 + self.core, self.field)

    def to_zl(self, k):
        other = lax.rem(self.zl + k, 4)
        return other, (self.x * 8 + other * 2 + self.core, self.field)

    def y_group(self):
        return [self.to_y(k)[1] for k in (1, 2, 3)]

    def field_group(self):
        return self.y_group() + [self.to_zh()[1]]

    def batch_group(self):
        return [self.to_core()[1]] + [self.to_x(k)[1] for k in (1, 2, 3)] + [self.to_zl(k)[1] for k in (1, 2, 3)]


def greet(peers):
    barrier = pltpu.get_barrier_semaphore()
    for peer in peers:
        pl.semaphore_signal(barrier, inc=1, device_id=peer, device_id_type=MESH)
    pl.semaphore_wait(barrier, len(peers))


def send(src, dst, sems, index, peer):
    copy = pltpu.make_async_remote_copy(
        src_ref=src,
        dst_ref=dst,
        send_sem=sems.at[0, index],
        recv_sem=sems.at[1, index],
        device_id=peer,
        device_id_type=MESH,
    )
    copy.start()
    return copy


def params(collective_id):
    return pltpu.CompilerParams(
        collective_id=collective_id, has_side_effects=True, vmem_limit_bytes=LIMIT
    )


def cost(us):
    return pl.CostEstimate(flops=0, bytes_accessed=int(us * 3.0e6), transcendentals=0)


def call(kernel, outs, scratch, collective_id, us, *args):
    return pl.pallas_call(
        kernel,
        out_shape=[jax.ShapeDtypeStruct(shape, dtype) for shape, dtype in outs],
        in_specs=[pl.BlockSpec(memory_space=VMEM)] * len(args),
        out_specs=[pl.BlockSpec(memory_space=VMEM)] * len(outs),
        scratch_shapes=scratch,
        compiler_params=params(collective_id),
        cost_estimate=cost(us),
    )(*args)


def rows(start, size):
    return pl.ds(pl.multiple_of(start * size, size), size)


def compress_kernel(part_ref, wl_ref, out_ref, wl_out, got, mine, other, sems):
    at = Place()
    greet(at.field_group())
    step = part_ref.shape[0] // 4
    copies, sends = [], []
    for k in (1, 2, 3):
        y, peer = at.to_y(k)
        copies.append(send(part_ref.at[rows(y, step)], got.at[k - 1], sems, k - 1, peer))
    for k in (1, 2, 3):
        peer = at.to_y(k)[1]
        sends.append(send(wl_ref, wl_out.at[k - 1], sems, 2 + k, peer))
    for copy in copies:
        copy.wait()
    own = rows(at.y, step)
    mine[...] = (
        part_ref[own].astype(F32) + got[0].astype(F32) + got[1].astype(F32) + got[2].astype(F32)
    ).astype(BF16)
    send(mine, other, sems, 6, at.to_zh()[1]).wait()
    out_ref[own] = (mine[...].astype(F32) + other[...].astype(F32)).astype(BF16)
    for k in (1, 2, 3):
        sends.append(send(out_ref.at[own], out_ref.at[own], sems, 6 + k, at.to_y(k)[1]))
    for copy in sends:
        copy.wait()


def reduce_rows(at, part_ref, got, mine, other, sems):
    step = part_ref.shape[0] // 4
    copies = []
    for k in (1, 2, 3):
        y, peer = at.to_y(k)
        copies.append(send(part_ref.at[rows(y, step)], got.at[k - 1], sems, k - 1, peer))
    for copy in copies:
        copy.wait()
    mine[...] = (
        part_ref[rows(at.y, step)].astype(F32)
        + got[0].astype(F32)
        + got[1].astype(F32)
        + got[2].astype(F32)
    ).astype(BF16)
    send(mine, other, sems, 3, at.to_zh()[1]).wait()
    return mine[...].astype(F32) + other[...].astype(F32)


def gather_rows(at, out_ref, sems):
    own = rows(at.y, out_ref.shape[0] // 4)
    return [send(out_ref.at[own], out_ref.at[own], sems, 3 + k, at.to_y(k)[1]) for k in (1, 2, 3)]


def hidden_kernel(part_ref, bias_ref, hidden_ref, pre_ref, got, mine, other, sems):
    at = Place()
    greet(at.field_group())
    pre = reduce_rows(at, part_ref, got, mine, other, sems) + bias_ref[...]
    pre_ref[...] = pre
    step = part_ref.shape[0] // 4
    hidden_ref[rows(at.y, step)] = (pre / (1.0 + jnp.exp(-pre))).astype(BF16)
    for copy in gather_rows(at, hidden_ref, sems):
        copy.wait()


def back_kernel(
    part_ref, pre_ref, lin_ref, grad_ref, bias_ref, raw_ref, got, mine, other, lmine, lother, sems, lsems
):
    at = Place()
    greet(at.field_group())
    half, fields = lin_ref.shape[0] // 2, raw_ref.shape[0]
    width = lin_ref.shape[1]
    zh, zpeer = at.to_zh()
    lcopies = []
    for j in range(4):
        lcopies.append(
            send(
                lin_ref.at[pl.ds(zh * half + j * fields, fields)],
                lother.at[pl.ds(j * fields, fields)],
                lsems,
                j,
                zpeer,
            )
        )
    total = reduce_rows(at, part_ref, got, mine, other, sems)
    pre = pre_ref[...]
    sigma = 1.0 / (1.0 + jnp.exp(-pre))
    grad = total * sigma * (1.0 + pre * (1.0 - sigma))
    bias_ref[...] = jnp.sum(grad.reshape(-1, 8, grad.shape[-1]), axis=0)
    step = part_ref.shape[0] // 4
    grad_ref[rows(at.y, step)] = grad.astype(BF16)
    sends = gather_rows(at, grad_ref, sems)
    for copy in lcopies:
        copy.wait()
    columns = rows(at.y, width)
    for n in range(half):
        lmine[n] = (lin_ref[at.zh * half + n].astype(F32) + lother[n].astype(F32)).astype(BF16)
    for k in (1, 2, 3):
        y, peer = at.to_y(k)
        sends.append(
            send(lmine.at[pl.ds(y * fields, fields)], raw_ref.at[:, columns, :], lsems, 3 + k, peer)
        )
    raw_ref[:, columns, :] = lmine[pl.ds(at.y * fields, fields)]
    for copy in sends:
        copy.wait()


def grads_kernel(
    scale,
    down_ref,
    up_ref,
    glc_ref,
    cb_ref,
    gather_ref,
    down_out,
    up_out,
    cgot,
    cmine,
    cother,
    d1,
    d2,
    d3,
    u1,
    u2,
    u3,
    ysems,
    zsems,
    csems,
    dsems,
    usems,
):
    at = Place()
    greet(at.field_group() + at.batch_group())
    fields, step = glc_ref.shape[0], gather_ref.shape[1]
    kk = cb_ref.shape[0]
    half = 4 * fields
    zpeer = at.to_zh()[1]
    zbase = at.zh * half
    sends = []
    weights = ((down_ref, d1, d2, d3, dsems, down_out), (up_ref, u1, u2, u3, usems, up_out))
    firsts = []
    core, cpeer = at.to_core()
    for ref, one, two, three, sems, out in weights:
        firsts.append(send(ref.at[:, core], one, sems, 0, cpeer))
    ccopies = []
    for k in (1, 2, 3):
        y, peer = at.to_y(k)
        ccopies.append(send(cb_ref.at[:, rows(y, step), :], cgot.at[k - 1], csems, k - 1, peer))
    gcopies = []
    for k in (1, 2, 3):
        y, peer = at.to_y(k)
        gcopies.append(
            send(
                glc_ref.at[:, rows(y, step), :],
                gather_ref.at[pl.ds(zbase + at.y * fields, fields)],
                ysems,
                k - 1,
                peer,
            )
        )
    own = pl.ds(zbase + at.y * fields, fields)
    gather_ref[own] = glc_ref[:, rows(at.y, step), :]
    zcopies = [send(gather_ref.at[own], gather_ref.at[own], zsems, 0, zpeer)]
    seconds = []
    for (ref, one, two, three, sems, out), first in zip(weights, firsts):
        first.wait()
        for j in range(16):
            one[j] = (one[j].astype(F32) + ref[j, at.core].astype(F32)).astype(BF16)
        group = []
        for k in (1, 2, 3):
            x, peer = at.to_x(k)
            group.append(send(one.at[pl.ds(x * 4, 4)], two.at[k - 1], sems, k, peer))
        seconds.append(group)
    for copy in ccopies:
        copy.wait()
    cmine[...] = (
        cb_ref[:, rows(at.y, step), :].astype(F32)
        + cgot[0].astype(F32)
        + cgot[1].astype(F32)
        + cgot[2].astype(F32)
    ).astype(BF16)
    ccopy = send(cmine, cother, csems, 3, zpeer)
    for k in (1, 2, 3):
        gcopies[k - 1].wait()
        source = lax.rem(at.y + 4 - k, 4)
        part = pl.ds(zbase + source * fields, fields)
        zcopies.append(send(gather_ref.at[part], gather_ref.at[part], zsems, k, zpeer))
    ccopy.wait()
    gather_ref[pl.ds(2 * half, kk)] = (
        (cmine[...].astype(F32) + cother[...].astype(F32)) * scale
    ).astype(BF16)
    thirds = []
    for (ref, one, two, three, sems, out), group in zip(weights, seconds):
        for copy in group:
            copy.wait()
        for j in range(4):
            total = one[at.x * 4 + j].astype(F32)
            for k in range(3):
                total = total + two[k, j].astype(F32)
            two[0, j] = total.astype(BF16)
        group = []
        for k in (1, 2, 3):
            z, peer = at.to_zl(k)
            group.append(send(two.at[0, z], three.at[k - 1], sems, 3 + k, peer))
        thirds.append(group)
    for (ref, one, two, three, sems, out), group in zip(weights, thirds):
        for copy in group:
            copy.wait()
        total = two[0, at.zl].astype(F32)
        for k in range(3):
            total = total + three[k].astype(F32)
        out[...] = total
    for copy in zcopies:
        copy.wait()


def small_kernel(part_ref, rows_ref, out_ref, ygot, rgot, rmine, rother, one, xmine, xgot, zmine, zgot, sems):
    at = Place()
    greet(at.field_group() + at.batch_group())
    fields, lanes = part_ref.shape[1:]
    copies = []
    for k in (1, 2, 3):
        peer = at.to_y(4 - k)[1]
        copies.append(send(part_ref.at[k], ygot.at[k - 1], sems, k - 1, peer))
        copies.append(send(rows_ref, rgot.at[k - 1], sems, 2 + k, peer))
    for copy in copies:
        copy.wait()
    rmine[...] = (rows_ref[...] + rgot[1]) + (rgot[0] + rgot[2])
    copy = send(rmine, rother, sems, 6, at.to_zh()[1])
    one[0, :fields] = part_ref[0] + ygot[0] + ygot[1] + ygot[2]
    copy.wait()
    one[0, fields:] = rmine[...] + rother[...]
    send(one.at[0], one.at[1], sems, 7, at.to_core()[1]).wait()
    xmine[...] = one[0] + one[1]
    copies = [send(xmine, xgot.at[k - 1], sems, 7 + k, at.to_x(k)[1]) for k in (1, 2, 3)]
    for copy in copies:
        copy.wait()
    zmine[...] = (xmine[...] + xgot[1]) + (xgot[0] + xgot[2])
    copies = [send(zmine, zgot.at[k - 1], sems, 10 + k, at.to_zl(k)[1]) for k in (1, 2, 3)]
    for copy in copies:
        copy.wait()
    out_ref[...] = (zmine[...] + zgot[1]) + (zgot[0] + zgot[2])


def norm_rows(values):
    centre = values - jnp.mean(values, axis=-1, keepdims=True)
    rstd = lax.rsqrt(jnp.mean(centre * centre, axis=-1, keepdims=True) + 1e-05)
    return (centre * rstd, rstd)


def norm_back(cotangent, normed, rstd, ln_gain):
    dn = cotangent * ln_gain
    return rstd * (
        dn
        - jnp.mean(dn, axis=-1, keepdims=True)
        - normed * jnp.mean(dn * normed, axis=-1, keepdims=True)
    )


def y_shift(k):
    return [
        (b * 8 + zh * 4 + y, b * 8 + zh * 4 + (y + k) % 4)
        for b in range(32)
        for zh in range(2)
        for y in range(4)
    ]


def local(embeddings, compress, w_up, up_bias, w_down, w_linear, ln_gain, cot_fm, cot_lc):
    examples, local_fields, width = embeddings.shape
    hidden_units, kk, nl = w_up.shape[0], compress.shape[1], w_linear.shape[1]
    part = width // 4
    quarter = examples // 4
    inv_root = float(width) ** (-0.5)
    y = lax.rem(lax.axis_index("field"), 4)
    turned = embeddings.transpose(1, 2, 0)

    slices = []
    for k in (0, 1, 2, 3):
        piece = lax.dynamic_slice_in_dim(turned, lax.rem(y + k, 4) * part, part, axis=1)
        slices.append(piece if k == 0 else lax.ppermute(piece, ("batch", "field"), y_shift(k)))

    comp_part = jnp.einsum("feb,fk->ekb", turned, compress, preferred_element_type=F32).astype(BF16)
    wl = jnp.pad(w_linear, ((0, 0), (0, 128 - nl)))
    compressed, wl_got = call(
        compress_kernel,
        [(comp_part.shape, BF16), ((3, local_fields, 128), BF16)],
        [
            VMEM((3, part, kk, examples), BF16),
            VMEM((part, kk, examples), BF16),
            VMEM((part, kk, examples), BF16),
            pltpu.SemaphoreType.DMA((2, 10)),
        ],
        0,
        30,
        comp_part,
        wl,
    )
    interact = (
        jnp.einsum("bfe,ekb->bfk", embeddings, compressed, preferred_element_type=F32) * inv_root
    ).astype(BF16)
    flat = interact.reshape(examples, -1)
    pre_part = jnp.einsum("bj,hj->bh", flat, w_up, preferred_element_type=F32).astype(BF16)
    row_scratch = [
        VMEM((3, quarter, hidden_units), BF16),
        VMEM((quarter, hidden_units), BF16),
        VMEM((quarter, hidden_units), BF16),
    ]
    hidden, hidden_pre = call(
        hidden_kernel,
        [((examples, hidden_units), BF16), ((quarter, hidden_units), F32)],
        row_scratch + [pltpu.SemaphoreType.DMA((2, 7))],
        1,
        15,
        pre_part,
        up_bias.reshape(1, -1),
    )
    fm_raw = jnp.dot(hidden, w_down, preferred_element_type=F32).reshape(examples, -1, width)
    fm_normed, fm_rstd = norm_rows(fm_raw)
    fm_out = (fm_normed * ln_gain).astype(BF16)
    cot_first = cot_fm.astype(F32)
    gain_local = jnp.sum(cot_first * fm_normed, axis=(0, 1))
    grad_fm = norm_back(cot_first, fm_normed, fm_rstd, ln_gain).astype(BF16).reshape(examples, -1)
    hidden_part = jnp.einsum("bc,hc->bh", grad_fm, w_down, preferred_element_type=F32).astype(BF16)

    lin = sum(
        jnp.einsum(
            "feb,fn->neb",
            slices[k],
            w_linear if k == 0 else wl_got[k - 1, :, :nl],
            preferred_element_type=F32,
        )
        for k in range(4)
    ).astype(BF16)
    out_fields = nl // 8
    grad_pre, bias_part, lc_raw = call(
        back_kernel,
        [
            ((examples, hidden_units), BF16),
            ((8, hidden_units), F32),
            ((out_fields, width, examples), BF16),
        ],
        row_scratch
        + [
            VMEM((nl // 2, part, examples), BF16),
            VMEM((nl // 2, part, examples), BF16),
            pltpu.SemaphoreType.DMA((2, 7)),
            pltpu.SemaphoreType.DMA((2, 7)),
        ],
        2,
        35,
        hidden_part,
        hidden_pre,
        lin,
    )
    lc_raw = lc_raw.transpose(2, 0, 1).astype(F32)
    lc_normed, lc_rstd = norm_rows(lc_raw)
    lc_out = (lc_normed * ln_gain).astype(BF16)
    cot_second = cot_lc.astype(F32)
    gain_local = gain_local + jnp.sum(cot_second * lc_normed, axis=(0, 1))
    grad_lc = norm_back(cot_second, lc_normed, lc_rstd, ln_gain).astype(BF16)

    down_part = jnp.einsum("bh,bc->hc", hidden, grad_fm, preferred_element_type=F32).astype(BF16)
    up_part = jnp.einsum("bh,bj->hj", grad_pre, flat, preferred_element_type=F32).astype(BF16)
    grad_inter = (
        jnp.dot(grad_pre, w_up, preferred_element_type=F32)
        .astype(BF16)
        .reshape(examples, local_fields, -1)
    )
    comp_back = jnp.einsum(
        "bfk,bfe->keb", grad_inter, embeddings, preferred_element_type=F32
    ).astype(BF16)
    own_rows = hidden_units // 32
    down_columns, up_columns = w_down.shape[1], w_up.shape[1]

    def stages(columns):
        return [
            VMEM((16, own_rows, columns), BF16),
            VMEM((3, 4, own_rows, columns), BF16),
            VMEM((3, own_rows, columns), BF16),
        ]

    gathered, grad_down, grad_up = call(
        functools.partial(grads_kernel, inv_root),
        [
            ((nl + kk, part, examples), BF16),
            ((own_rows, down_columns), F32),
            ((own_rows, up_columns), F32),
        ],
        [
            VMEM((3, kk, part, examples), BF16),
            VMEM((kk, part, examples), BF16),
            VMEM((kk, part, examples), BF16),
        ]
        + stages(down_columns)
        + stages(up_columns)
        + [
            pltpu.SemaphoreType.DMA((2, 3)),
            pltpu.SemaphoreType.DMA((2, 4)),
            pltpu.SemaphoreType.DMA((2, 4)),
            pltpu.SemaphoreType.DMA((2, 7)),
            pltpu.SemaphoreType.DMA((2, 7)),
        ],
        3,
        60,
        down_part.reshape(16, 2, own_rows, down_columns),
        up_part.reshape(16, 2, own_rows, up_columns),
        grad_lc.transpose(1, 2, 0),
        comp_back,
    )
    mixed = jnp.stack(
        [
            jnp.einsum("feb,neb->fn", slices[k], gathered, preferred_element_type=F32)
            for k in range(4)
        ]
    )
    mixed = jnp.pad(mixed, ((0, 0), (0, 0), (0, 128 - nl - kk)))
    bias_rows = 0.5 * jnp.sum(bias_part, axis=0).reshape(-1, 128)
    gain_rows = jnp.pad(gain_local, (0, 256 - width)).reshape(-1, 128)
    extra = jnp.concatenate([bias_rows, gain_rows])
    n_extra = 16
    extra = jnp.pad(extra, ((0, n_extra - extra.shape[0]), (0, 0)))
    total_rows = local_fields + n_extra
    (sums,) = call(
        small_kernel,
        [((total_rows, 128), F32)],
        [
            VMEM((3, local_fields, 128), F32),
            VMEM((3, n_extra, 128), F32),
            VMEM((n_extra, 128), F32),
            VMEM((n_extra, 128), F32),
            VMEM((2, total_rows, 128), F32),
            VMEM((total_rows, 128), F32),
            VMEM((3, total_rows, 128), F32),
            VMEM((total_rows, 128), F32),
            VMEM((3, total_rows, 128), F32),
            pltpu.SemaphoreType.DMA((2, 14)),
        ],
        4,
        20,
        mixed,
        extra,
    )
    grad_linear = sums[:local_fields, :nl]
    grad_compress = sums[:local_fields, nl : nl + kk]
    n_bias = hidden_units // 128
    grad_bias = sums[local_fields : local_fields + n_bias].reshape(-1)
    grad_gain = sums[local_fields + n_bias : local_fields + n_bias + 2].reshape(-1)[:width]
    return (fm_out, lc_out, grad_compress, grad_up, grad_bias, grad_down, grad_linear, grad_gain)


def solution(mesh):
    placed = (
        P("batch", "field", None),
        P("field", None),
        P(None, "field"),
        P(),
        P(None, "field"),
        P("field", None),
        P(),
        P("batch", "field", None),
        P("batch", "field", None),
    )
    return jax.shard_map(
        local,
        mesh=mesh,
        in_specs=placed,
        out_specs=(
            P("batch", "field", None),
            P("batch", "field", None),
            P("field", None),
            P("batch", "field"),
            P(),
            P("batch", "field"),
            P("field", None),
            P(),
        ),
        check_vma=False,
    )
```

```python
import functools

import jax
import jax.numpy as jnp
from jax import lax
from jax.experimental import pallas as pl
from jax.experimental.pallas import tpu as pltpu
from jax.sharding import PartitionSpec as P

MESH = pl.DeviceIdType.MESH
VMEM = pltpu.VMEM
F32 = jnp.float32
BF16 = jnp.bfloat16
LIMIT = 24 * 1024 * 1024


class Place:
    def __init__(self):
        batch, field = lax.axis_index("batch"), lax.axis_index("field")
        self.batch, self.field = batch, field
        self.y, self.zh = lax.rem(field, 4), lax.div(field, 4)
        self.core = lax.rem(batch, 2)
        self.zl = lax.rem(lax.div(batch, 2), 4)
        self.x = lax.div(batch, 8)

    def to_y(self, k):
        other = lax.rem(self.y + k, 4)
        return other, (self.batch, self.zh * 4 + other)

    def to_zh(self):
        other = 1 - self.zh
        return other, (self.batch, other * 4 + self.y)

    def to_core(self):
        other = 1 - self.core
        return other, (self.x * 8 + self.zl * 2 + other, self.field)

    def to_x(self, k):
        other = lax.rem(self.x + k, 4)
        return other, (other * 8 + self.zl * 2 + self.core, self.field)

    def to_zl(self, k):
        other = lax.rem(self.zl + k, 4)
        return other, (self.x * 8 + other * 2 + self.core, self.field)

    def y_group(self):
        return [self.to_y(k)[1] for k in (1, 2, 3)]

    def field_group(self):
        return self.y_group() + [self.to_zh()[1]]

    def batch_group(self):
        return [self.to_core()[1]] + [self.to_x(k)[1] for k in (1, 2, 3)] + [self.to_zl(k)[1] for k in (1, 2, 3)]


def greet(peers, work=None):
    barrier = pltpu.get_barrier_semaphore()
    for peer in peers:
        pl.semaphore_signal(barrier, inc=1, device_id=peer, device_id_type=MESH)
    if work is not None:
        work()
    pl.semaphore_wait(barrier, len(peers))


def send(src, dst, sems, index, peer):
    copy = pltpu.make_async_remote_copy(
        src_ref=src,
        dst_ref=dst,
        send_sem=sems.at[0, index],
        recv_sem=sems.at[1, index],
        device_id=peer,
        device_id_type=MESH,
    )
    copy.start()
    return copy


def params(collective_id):
    return pltpu.CompilerParams(
        collective_id=collective_id, has_side_effects=True, vmem_limit_bytes=LIMIT
    )


def cost(us):
    return pl.CostEstimate(flops=0, bytes_accessed=int(us * 3.0e6), transcendentals=0)


def call(kernel, outs, scratch, collective_id, us, *args):
    return pl.pallas_call(
        kernel,
        out_shape=[jax.ShapeDtypeStruct(shape, dtype) for shape, dtype in outs],
        in_specs=[pl.BlockSpec(memory_space=VMEM)] * len(args),
        out_specs=[pl.BlockSpec(memory_space=VMEM)] * len(outs),
        scratch_shapes=scratch,
        compiler_params=params(collective_id),
        cost_estimate=cost(us),
    )(*args)


def rows(start, size):
    return pl.ds(pl.multiple_of(start * size, size), size)


def field_sum(at, part_ref, got, mine, other, sems, between):
    step = part_ref.shape[0] // 4
    copies = []
    for k in (1, 2, 3):
        y, peer = at.to_y(k)
        copies.append(send(part_ref.at[rows(y, step)], got.at[k - 1], sems, k - 1, peer))
    for copy in copies:
        copy.wait()
    mine[...] = (
        part_ref[rows(at.y, step)].astype(F32)
        + got[0].astype(F32)
        + got[1].astype(F32)
        + got[2].astype(F32)
    ).astype(BF16)
    copy = send(mine, other, sems, 3, at.to_zh()[1])
    between()
    copy.wait()
    return mine[...].astype(F32) + other[...].astype(F32)


def gather_rows(at, out_ref, sems):
    own = rows(at.y, out_ref.shape[0] // 4)
    return [send(out_ref.at[own], out_ref.at[own], sems, 3 + k, at.to_y(k)[1]) for k in (1, 2, 3)]


def mean0(values):
    return jnp.sum(values, axis=0, keepdims=True) * (1.0 / values.shape[0])


def norm(raw, cot, gain):
    centre = raw - mean0(raw)
    rstd = lax.rsqrt(mean0(centre * centre) + 1e-05)
    normed = centre * rstd
    dn = cot * gain
    grad = rstd * (dn - mean0(dn) - normed * mean0(dn * normed))
    return normed * gain, cot * normed, grad


def front_kernel(
    pieces,
    part_ref,
    wl_ref,
    emb_ref,
    up_ref,
    bias_ref,
    wl_out,
    emb_out,
    flat_ref,
    hidden_ref,
    pre_ref,
    cgot,
    cmine,
    cother,
    comp,
    compf,
    embf,
    part,
    got,
    mine,
    other,
    csems,
    wsems,
    esems,
    psems,
):
    at = Place()
    fields, width, examples = emb_ref.shape
    step, kk = width // 4, part_ref.shape[1]
    scale = float(width) ** (-0.5)
    block = embf.shape[0]
    size = fields // pieces
    background = []

    def piece(p):
        here = pl.ds(p * size, size)
        for k in (1, 2, 3):
            y, peer = at.to_y(k)
            background.append(
                send(emb_ref.at[here, rows(y, step), :], emb_out.at[k, here], esems, p * 3 + k - 1, peer)
            )

    def own_part():
        wl_out[0] = jnp.zeros(wl_out.shape[1:], BF16)
        wl_out[0, :, : wl_ref.shape[1]] = wl_ref[...]
        emb_out[0] = emb_ref[:, rows(at.y, step), :]

    greet(at.field_group(), own_part)
    copies = []
    for k in (1, 2, 3):
        y, peer = at.to_y(k)
        copies.append(send(part_ref.at[rows(y, step)], cgot.at[k - 1], csems, k - 1, peer))
    for k in (1, 2, 3):
        background.append(send(wl_out.at[0], wl_out.at[k], wsems, k - 1, at.to_y(k)[1]))
    for copy in copies:
        copy.wait()
    cmine[...] = (
        part_ref[rows(at.y, step)].astype(F32)
        + cgot[0].astype(F32)
        + cgot[1].astype(F32)
        + cgot[2].astype(F32)
    ).astype(BF16)
    copy = send(cmine, cother, csems, 3, at.to_zh()[1])
    piece(0)
    piece(1)
    copy.wait()
    own = rows(at.y, step)
    comp[own] = (cmine[...].astype(F32) + cother[...].astype(F32)).astype(BF16)
    copies = [send(comp.at[own], comp.at[own], csems, 3 + k, at.to_y(k)[1]) for k in (1, 2, 3)]
    for copy in copies:
        copy.wait()
    compf[...] = comp[...].astype(F32)

    def interact(start, stop):
        @pl.loop(start, stop)
        def _(i):
            embf[...] = emb_ref[pl.ds(i * block, block)].astype(F32)

            def terms(e, totals):
                c = compf[e]
                return tuple(t + c * embf[j, pl.ds(e, 1), :] for j, t in enumerate(totals))

            totals = lax.fori_loop(
                0, width, terms, tuple(jnp.zeros((kk, examples), F32) for _ in range(block)), unroll=8
            )
            for j in range(block):
                flat_ref[i * block + j] = (totals[j] * scale).astype(BF16)

    blocks = fields // block
    cuts = [blocks * p // 3 for p in range(4)]
    for p in range(3):
        piece(2 + p)
        interact(cuts[p], cuts[p + 1])

    flat = flat_ref[...].reshape(fields * kk, examples)
    units = up_ref.shape[0]
    quarter = units // 4

    @pl.loop(0, 4)
    def _(r):
        part[rows(r, quarter)] = jnp.dot(
            up_ref[rows(r, quarter), :], flat, preferred_element_type=F32
        ).astype(BF16)

    def after(p):
        def go():
            if p < pieces:
                piece(p)

        return go

    bias = jnp.transpose(jnp.broadcast_to(bias_ref[:, rows(at.y, quarter)], (examples, quarter)))
    pre = field_sum(at, part, got, mine, other, psems, after(5)) + bias
    pre_ref[...] = pre
    hidden_ref[rows(at.y, quarter)] = (pre / (1.0 + jnp.exp(-pre))).astype(BF16)
    for copy in gather_rows(at, hidden_ref, psems):
        copy.wait()
    for copy in background:
        copy.wait()


class BatchSum:
    def __init__(self, at, ref, one, two, three, sems, out):
        self.at, self.ref, self.one, self.two, self.three, self.sems, self.out = (
            at, ref, one, two, three, sems, out,
        )

    def first(self):
        core, peer = self.at.to_core()
        self.copies = [send(self.ref.at[:, core], self.one, self.sems, 0, peer)]

    def wait(self):
        for copy in self.copies:
            copy.wait()

    def second(self):
        self.wait()
        one = self.one

        @pl.loop(0, 16)
        def _(j):
            one[j] = (one[j].astype(F32) + self.ref[j, self.at.core].astype(F32)).astype(BF16)

        self.copies = []
        for k in (1, 2, 3):
            x, peer = self.at.to_x(k)
            self.copies.append(send(one.at[pl.ds(x * 4, 4)], self.two.at[k - 1], self.sems, k, peer))

    def third(self):
        self.wait()
        for j in range(4):
            total = self.one[self.at.x * 4 + j].astype(F32)
            for k in range(3):
                total = total + self.two[k, j].astype(F32)
            self.two[0, j] = total.astype(BF16)
        self.copies = []
        for k in (1, 2, 3):
            z, peer = self.at.to_zl(k)
            self.copies.append(send(self.two.at[0, z], self.three.at[k - 1], self.sems, 3 + k, peer))

    def last(self):
        self.wait()
        total = self.two[0, self.at.zl].astype(F32)
        for k in range(3):
            total = total + self.three[k].astype(F32)
        self.out[...] = total


def middle_kernel(
    hidden_ref,
    pre_ref,
    down_ref,
    cot_ref,
    gain_ref,
    lin_ref,
    fm_ref,
    gain_out,
    gpre_ref,
    bias_out,
    raw_ref,
    down_out,
    gfm_ref,
    part,
    got,
    mine,
    other,
    lmine,
    lother,
    dpart,
    d1,
    d2,
    d3,
    hsems,
    lsems,
    dsems,
):
    at = Place()
    units, examples = hidden_ref.shape
    width, quarter = gain_ref.shape[0], units // 4
    chunk, step = raw_ref.shape[0], raw_ref.shape[1] // 4
    half = 4 * chunk
    zh, zpeer = at.to_zh()
    lcopies = []

    def linear(j):
        field = lax.rem(at.y + 1 + j, 4) * chunk
        lcopies.append(
            send(lin_ref.at[pl.ds(zh * half + field, chunk)], lother.at[pl.ds(field, chunk)], lsems, j, zpeer)
        )

    gain = gain_ref[...]

    def forward():
        hidden = jnp.transpose(hidden_ref[...].astype(F32)).astype(BF16)
        gain_total = jnp.zeros((width, examples), F32)
        for n in range(0, cot_ref.shape[0], 2):
            raw = jnp.transpose(
                jnp.dot(hidden, down_ref[:, n * width : (n + 2) * width], preferred_element_type=F32)
            )
            for m in range(2):
                out, term, grad = norm(
                    raw[m * width : (m + 1) * width], cot_ref[n + m].astype(F32), gain
                )
                fm_ref[n + m] = out.astype(BF16)
                gain_total = gain_total + term
                gfm_ref[n + m] = grad.astype(BF16)
        gain_out[...] = gain_total

    greet(at.field_group() + at.batch_group(), forward)
    linear(0)
    linear(1)
    gfm = gfm_ref[...].reshape(down_ref.shape[1], examples)

    @pl.loop(0, 4)
    def _(r):
        part[rows(r, quarter)] = jnp.dot(
            down_ref[rows(r, quarter), :], gfm, preferred_element_type=F32
        ).astype(BF16)

    copies = []
    for k in (1, 2, 3):
        y, peer = at.to_y(k)
        copies.append(send(part.at[rows(y, quarter)], got.at[k - 1], hsems, k - 1, peer))

    @pl.loop(0, 4)
    def _(r):
        block = lax.dot_general(
            hidden_ref[rows(r, quarter), :],
            gfm,
            (((1,), (1,)), ((), ())),
            preferred_element_type=F32,
        ).astype(BF16)
        dpart[rows(r, 4)] = block.reshape((4,) + dpart.shape[1:])

    down = BatchSum(at, dpart, d1, d2, d3, dsems, down_out)
    down.first()
    for copy in copies:
        copy.wait()
    mine[...] = (
        part[rows(at.y, quarter)].astype(F32)
        + got[0].astype(F32)
        + got[1].astype(F32)
        + got[2].astype(F32)
    ).astype(BF16)
    copy = send(mine, other, hsems, 3, zpeer)
    linear(2)
    linear(3)
    down.second()
    pre = pre_ref[...]
    sigma = 1.0 / (1.0 + jnp.exp(-pre))
    slope = sigma * (1.0 + pre * (1.0 - sigma))
    copy.wait()
    grad = (mine[...].astype(F32) + other[...].astype(F32)) * slope
    gpre_ref[rows(at.y, quarter)] = grad.astype(BF16)
    copies = gather_rows(at, gpre_ref, hsems)
    bias_out[...] = jnp.sum(grad, axis=1, keepdims=True)
    zbase = at.zh * half
    own = rows(at.y, step)
    for j in range(4):
        lcopies[j].wait()
        field, peer = at.to_y(j + 1)
        for n in range(chunk):
            lmine[field * chunk + n] = (
                lin_ref[zbase + field * chunk + n].astype(F32) + lother[field * chunk + n].astype(F32)
            ).astype(BF16)
        if j < 3:
            copies.append(
                send(lmine.at[pl.ds(field * chunk, chunk)], raw_ref.at[:, own, :], lsems, 4 + j, peer)
            )
        if j == 1:
            down.third()
    raw_ref[:, own, :] = lmine[pl.ds(at.y * chunk, chunk)]
    down.last()
    for copy in copies:
        copy.wait()


def grads_kernel(
    raw,
    up_ref,
    inter_ref,
    emb_ref,
    cot_ref,
    gain_ref,
    rows_ref,
    out_ref,
    gather_ref,
    gcomp_ref,
    up_out,
    rows_out,
    interf,
    embf,
    cb,
    cgot,
    cmine,
    cother,
    glc,
    u1,
    u2,
    u3,
    rgot,
    rmine,
    rsum,
    rother,
    ysems,
    zsems,
    csems,
    usems,
    rsems,
):
    at = Place()
    fields, width, examples = emb_ref.shape
    kk, step = inter_ref.shape[1], width // 4
    scale = float(width) ** (-0.5)
    out_fields = cot_ref.shape[0]
    half = 4 * out_fields
    zh, zpeer = at.to_zh()
    zbase = at.zh * half
    own_part = rows(at.y, step)
    gain = gain_ref[...]

    def linear():
        rsum[...] = jnp.zeros_like(rsum)

        @pl.loop(0, out_fields)
        def _(n):
            out, term, grad = norm(raw[n].astype(F32), cot_ref[n].astype(F32), gain)
            out_ref[n] = out.astype(BF16)
            rsum[...] += term
            glc[n] = grad.astype(BF16)

    greet(at.field_group() + at.batch_group(), linear)
    own = pl.ds(zbase + at.y * out_fields, out_fields)
    gcopies = []
    for k in (1, 2, 3):
        y, peer = at.to_y(k)
        gcopies.append(send(glc.at[:, rows(y, step), :], gather_ref.at[own], ysems, k - 1, peer))
    gather_ref[own] = glc[:, own_part, :]
    zcopies = [send(gather_ref.at[own], gather_ref.at[own], zsems, 0, zpeer)]
    n_bias = rows_ref.shape[0] - 4
    rmine[...] = rows_ref[...]
    rmine[n_bias : n_bias + 1, :width] = rmine[n_bias : n_bias + 1, :width] + jnp.sum(
        jnp.transpose(rsum[...]), axis=0, keepdims=True
    )
    rcopies = [send(rmine, rgot.at[k - 1], rsems, k - 1, at.to_y(k)[1]) for k in (1, 2, 3)]
    up = BatchSum(at, up_ref, u1, u2, u3, usems, up_out)
    up.first()
    interf[...] = inter_ref[...].astype(F32)
    block = embf.shape[1]

    def compression(start, stop):
        @pl.loop(start, stop)
        def _(i):
            embf[...] = emb_ref[:, rows(i, block), :].astype(F32)

            def terms(f, totals):
                g = interf[f]
                return tuple(t + g * embf[f, pl.ds(j, 1), :] for j, t in enumerate(totals))

            totals = lax.fori_loop(
                0, fields, terms, tuple(jnp.zeros((kk, examples), F32) for _ in range(block)), unroll=4
            )
            for j in range(block):
                cb[i * block + j] = totals[j].astype(BF16)

    blocks = width // block
    compression(0, blocks // 3)
    up.second()
    for k in (1, 2, 3):
        gcopies[k - 1].wait()
        source = lax.rem(at.y + 4 - k, 4)
        there = pl.ds(zbase + source * out_fields, out_fields)
        zcopies.append(send(gather_ref.at[there], gather_ref.at[there], zsems, k, zpeer))
    for copy in rcopies:
        copy.wait()
    rmine[...] = (rmine[...] + rgot[1]) + (rgot[0] + rgot[2])
    rcopy = send(rmine, rother, rsems, 3, zpeer)
    compression(blocks // 3, blocks)
    ccopies = []
    for k in (1, 2, 3):
        y, peer = at.to_y(k)
        ccopies.append(send(cb.at[rows(y, step)], cgot.at[k - 1], csems, k - 1, peer))
    for copy in ccopies:
        copy.wait()
    cmine[...] = (
        cb[own_part].astype(F32)
        + cgot[0].astype(F32)
        + cgot[1].astype(F32)
        + cgot[2].astype(F32)
    ).astype(BF16)
    ccopy = send(cmine, cother, csems, 3, zpeer)
    up.third()
    rcopy.wait()
    rows_out[...] = rmine[...] + rother[...]
    ccopy.wait()
    gcomp_ref[...] = ((cmine[...].astype(F32) + cother[...].astype(F32)) * scale).astype(BF16)
    up.last()
    for copy in zcopies:
        copy.wait()


def small_kernel(
    nl, part_ref, rows_ref, lin_ref, comp_ref, rows_out, psend, ygot, one, xmine, xgot, zmine, zgot, sems
):
    at = Place()
    fields, kk = lin_ref.shape[0], comp_ref.shape[0]
    psend[...] = part_ref[...].astype(BF16)
    greet(at.y_group() + at.batch_group())
    copies = []
    for k in (1, 2, 3):
        copies.append(send(psend.at[k], ygot.at[k - 1], sems, k - 1, at.to_y(4 - k)[1]))
    half = rows_ref.shape[0]
    one[0, fields : fields + half] = rows_ref[:, :128]
    one[0, fields + half :] = rows_ref[:, 128:]
    for copy in copies:
        copy.wait()
    one[0, :fields] = (
        part_ref[0] + ygot[0].astype(F32) + ygot[1].astype(F32) + ygot[2].astype(F32)
    )
    send(one.at[0], one.at[1], sems, 3, at.to_core()[1]).wait()
    xmine[...] = (one[0] + one[1]).astype(BF16)
    copies = [send(xmine, xgot.at[k - 1], sems, 3 + k, at.to_x(k)[1]) for k in (1, 2, 3)]
    for copy in copies:
        copy.wait()
    zmine[...] = (
        (xmine[...].astype(F32) + xgot[1].astype(F32))
        + (xgot[0].astype(F32) + xgot[2].astype(F32))
    ).astype(BF16)
    copies = [send(zmine, zgot.at[k - 1], sems, 6 + k, at.to_zl(k)[1]) for k in (1, 2, 3)]
    for copy in copies:
        copy.wait()
    total = (zmine[...].astype(F32) + zgot[1].astype(F32)) + (
        zgot[0].astype(F32) + zgot[2].astype(F32)
    )
    lin_ref[...] = total[:fields, :nl]
    comp_ref[...] = jnp.transpose(total[:fields])[nl : nl + kk]
    rows_out[:, :128] = total[fields : fields + half]
    rows_out[:, 128:] = total[fields + half :]


def local(embeddings, compress, w_up, up_bias, w_down, w_linear, ln_gain, cot_fm, cot_lc):
    examples, fields, width = embeddings.shape
    units, kk, nl = w_up.shape[0], compress.shape[1], w_linear.shape[1]
    part, quarter, own_rows = width // 4, units // 4, units // 32
    turned = embeddings.transpose(1, 2, 0)
    gain = jnp.broadcast_to(ln_gain.reshape(-1, 1), (width, examples))
    comp_part = jnp.einsum("feb,fk->ekb", turned, compress, preferred_element_type=F32).astype(BF16)
    cot_first, cot_second = cot_fm.transpose(1, 2, 0), cot_lc.transpose(1, 2, 0)
    pieces, block = 6, 8

    def stages(columns):
        return [
            VMEM((16, own_rows, columns), BF16),
            VMEM((3, 4, own_rows, columns), BF16),
            VMEM((3, own_rows, columns), BF16),
        ]

    row_scratch = [
        VMEM((units, examples), BF16),
        VMEM((3, quarter, examples), BF16),
        VMEM((quarter, examples), BF16),
        VMEM((quarter, examples), BF16),
    ]
    wl_all, spread, flat, hidden, hidden_pre = call(
        functools.partial(front_kernel, pieces),
        [
            ((4, fields, 128), BF16),
            ((4, fields, part, examples), BF16),
            ((fields, kk, examples), BF16),
            ((units, examples), BF16),
            ((quarter, examples), F32),
        ],
        [
            VMEM((3, part, kk, examples), BF16),
            VMEM((part, kk, examples), BF16),
            VMEM((part, kk, examples), BF16),
            VMEM((width, kk, examples), BF16),
            VMEM((width, kk, examples), F32),
            VMEM((block, width, examples), F32),
        ]
        + row_scratch
        + [
            pltpu.SemaphoreType.DMA((2, 7)),
            pltpu.SemaphoreType.DMA((2, 3)),
            pltpu.SemaphoreType.DMA((2, 3 * pieces)),
            pltpu.SemaphoreType.DMA((2, 7)),
        ],
        0,
        80,
        comp_part,
        w_linear,
        turned,
        w_up,
        up_bias.reshape(1, -1),
    )
    spread = spread.reshape(4 * fields, part, examples)
    lin = jnp.einsum(
        "feb,fn->neb", spread, wl_all.reshape(4 * fields, 128)[:, :nl], preferred_element_type=F32
    ).astype(BF16)
    columns = cot_first.shape[0] * width
    fm_out, gain_fm, grad_pre, bias_part, lc_raw, grad_down = call(
        middle_kernel,
        [
            (cot_first.shape, BF16),
            ((width, examples), F32),
            ((units, examples), BF16),
            ((quarter, 1), F32),
            (cot_second.shape, BF16),
            ((own_rows, columns), F32),
        ],
        [VMEM(cot_first.shape, BF16)]
        + row_scratch
        + [
            VMEM((nl // 2, part, examples), BF16),
            VMEM((nl // 2, part, examples), BF16),
            VMEM((16, 2, own_rows, columns), BF16),
        ]
        + stages(columns)
        + [
            pltpu.SemaphoreType.DMA((2, 7)),
            pltpu.SemaphoreType.DMA((2, 7)),
            pltpu.SemaphoreType.DMA((2, 7)),
        ],
        1,
        35,
        hidden,
        hidden_pre,
        w_down,
        cot_first,
        gain,
        lin,
    )
    flat = flat.reshape(fields * kk, examples)
    up_part = jnp.einsum("hb,jb->hj", grad_pre, flat, preferred_element_type=F32).astype(BF16)
    grad_inter = (
        jnp.einsum("hj,hb->jb", w_up, grad_pre, preferred_element_type=F32)
        .astype(BF16)
        .reshape(fields, kk, examples)
    )
    n_bias = units // 256
    y = lax.rem(lax.axis_index("field"), 4)
    bias_rows = lax.dynamic_update_slice_in_dim(
        jnp.zeros((units,), F32), 0.5 * bias_part.reshape(-1), y * quarter, axis=0
    ).reshape(n_bias, 256)
    gain_row = jnp.pad(jnp.sum(gain_fm, axis=1), (0, 256 - width)).reshape(1, 256)
    extra = jnp.pad(jnp.concatenate([bias_rows, gain_row]), ((0, 3), (0, 0)))

    out_fields, n_extra, slab = nl // 8, extra.shape[0], 16
    lc_out, gathered, grad_comp, grad_up, extra = call(
        grads_kernel,
        [
            (cot_second.shape, BF16),
            ((nl, part, examples), BF16),
            ((part, kk, examples), BF16),
            ((own_rows, fields * kk), F32),
            (extra.shape, F32),
        ],
        [
            VMEM((fields, kk, examples), F32),
            VMEM((fields, slab, examples), F32),
            VMEM((width, kk, examples), BF16),
            VMEM((3, part, kk, examples), BF16),
            VMEM((part, kk, examples), BF16),
            VMEM((part, kk, examples), BF16),
            VMEM(cot_second.shape, BF16),
        ]
        + stages(fields * kk)
        + [
            VMEM((3,) + extra.shape, F32),
            VMEM(extra.shape, F32),
            VMEM((width, examples), F32),
            VMEM(extra.shape, F32),
            pltpu.SemaphoreType.DMA((2, 3)),
            pltpu.SemaphoreType.DMA((2, 4)),
            pltpu.SemaphoreType.DMA((2, 4)),
            pltpu.SemaphoreType.DMA((2, 7)),
            pltpu.SemaphoreType.DMA((2, 4)),
        ],
        2,
        45,
        lc_raw,
        up_part.reshape(16, 2, own_rows, fields * kk),
        grad_inter,
        turned,
        cot_second,
        gain,
        extra,
    )
    mixed = jnp.concatenate(
        [
            jnp.einsum("feb,neb->fn", spread, gathered, preferred_element_type=F32),
            jnp.einsum("feb,ekb->fk", spread, grad_comp, preferred_element_type=F32),
            jnp.zeros((4 * fields, 128 - nl - kk), F32),
        ],
        axis=1,
    ).reshape(4, fields, 128)
    total_rows = fields + 2 * n_extra
    grad_linear, grad_compress, extra = call(
        functools.partial(small_kernel, nl),
        [((fields, nl), F32), ((kk, fields), F32), (extra.shape, F32)],
        [
            VMEM((4, fields, 128), BF16),
            VMEM((3, fields, 128), BF16),
            VMEM((2, total_rows, 128), F32),
            VMEM((total_rows, 128), BF16),
            VMEM((3, total_rows, 128), BF16),
            VMEM((total_rows, 128), BF16),
            VMEM((3, total_rows, 128), BF16),
            pltpu.SemaphoreType.DMA((2, 10)),
        ],
        3,
        15,
        mixed,
        extra,
    )
    grad_bias = extra[:n_bias].reshape(-1)
    grad_gain = extra[n_bias, :width]
    return (
        fm_out.transpose(2, 0, 1),
        lc_out.transpose(2, 0, 1),
        grad_compress.T,
        grad_up,
        grad_bias,
        grad_down,
        grad_linear,
        grad_gain,
    )


def solution(mesh):
    placed = (
        P("batch", "field", None),
        P("field", None),
        P(None, "field"),
        P(),
        P(None, "field"),
        P("field", None),
        P(),
        P("batch", "field", None),
        P("batch", "field", None),
    )
    return jax.shard_map(
        local,
        mesh=mesh,
        in_specs=placed,
        out_specs=(
            P("batch", "field", None),
            P("batch", "field", None),
            P("field", None),
            P("batch", "field"),
            P(),
            P("batch", "field"),
            P("field", None),
            P(),
        ),
        check_vma=False,
    )
```

```python
import functools

import jax
import jax.numpy as jnp
from jax import lax
from jax.experimental import pallas as pl
from jax.experimental.pallas import tpu as pltpu
from jax.sharding import PartitionSpec as P

MESH = pl.DeviceIdType.MESH
VMEM = pltpu.VMEM
F32 = jnp.float32
BF16 = jnp.bfloat16
MIB = 1024 * 1024


class Place:
    def __init__(self):
        batch, field = lax.axis_index("batch"), lax.axis_index("field")
        self.batch, self.field = batch, field
        self.y, self.zh = lax.rem(field, 4), lax.div(field, 4)
        self.core = lax.rem(batch, 2)
        self.zl = lax.rem(lax.div(batch, 2), 4)
        self.x = lax.div(batch, 8)

    def to_y(self, k):
        other = lax.rem(self.y + k, 4)
        return other, (self.batch, self.zh * 4 + other)

    def to_zh(self):
        other = 1 - self.zh
        return other, (self.batch, other * 4 + self.y)

    def to_core(self):
        other = 1 - self.core
        return other, (self.x * 8 + self.zl * 2 + other, self.field)

    def to_x(self, k):
        other = lax.rem(self.x + k, 4)
        return other, (other * 8 + self.zl * 2 + self.core, self.field)

    def to_zl(self, k):
        other = lax.rem(self.zl + k, 4)
        return other, (self.x * 8 + other * 2 + self.core, self.field)

    def y_group(self):
        return [self.to_y(k)[1] for k in (1, 2, 3)]

    def field_group(self):
        return self.y_group() + [self.to_zh()[1]]

    def batch_group(self):
        return [self.to_core()[1]] + [self.to_x(k)[1] for k in (1, 2, 3)] + [self.to_zl(k)[1] for k in (1, 2, 3)]


def greet(peers, work=None):
    barrier = pltpu.get_barrier_semaphore()
    for peer in peers:
        pl.semaphore_signal(barrier, inc=1, device_id=peer, device_id_type=MESH)
    if work is not None:
        work()
    pl.semaphore_wait(barrier, len(peers))


def send(src, dst, sems, index, peer):
    copy = pltpu.make_async_remote_copy(
        src_ref=src,
        dst_ref=dst,
        send_sem=sems.at[0, index],
        recv_sem=sems.at[1, index],
        device_id=peer,
        device_id_type=MESH,
    )
    copy.start()
    return copy


def params(collective_id, mib):
    return pltpu.CompilerParams(
        collective_id=collective_id, has_side_effects=True, vmem_limit_bytes=mib * MIB
    )


def cost(us):
    return pl.CostEstimate(flops=0, bytes_accessed=int(us * 3.0e6), transcendentals=0)


def call(kernel, outs, scratch, collective_id, us, mib, *args):
    return pl.pallas_call(
        kernel,
        out_shape=[jax.ShapeDtypeStruct(shape, dtype) for shape, dtype in outs],
        in_specs=[pl.BlockSpec(memory_space=VMEM)] * len(args),
        out_specs=[pl.BlockSpec(memory_space=VMEM)] * len(outs),
        scratch_shapes=scratch,
        compiler_params=params(collective_id, mib),
        cost_estimate=cost(us),
    )(*args)


def rows(start, size):
    return pl.ds(pl.multiple_of(start * size, size), size)


def field_sum(at, part_ref, got, mine, other, sems, between):
    step = part_ref.shape[0] // 4
    copies = []
    for k in (1, 2, 3):
        y, peer = at.to_y(k)
        copies.append(send(part_ref.at[rows(y, step)], got.at[k - 1], sems, k - 1, peer))
    for copy in copies:
        copy.wait()
    mine[...] = (
        part_ref[rows(at.y, step)].astype(F32)
        + got[0].astype(F32)
        + got[1].astype(F32)
        + got[2].astype(F32)
    ).astype(BF16)
    copy = send(mine, other, sems, 3, at.to_zh()[1])
    between()
    copy.wait()
    return mine[...].astype(F32) + other[...].astype(F32)


def gather_rows(at, out_ref, sems):
    own = rows(at.y, out_ref.shape[0] // 4)
    return [send(out_ref.at[own], out_ref.at[own], sems, 3 + k, at.to_y(k)[1]) for k in (1, 2, 3)]


def mean0(values):
    return jnp.sum(values, axis=0, keepdims=True) * (1.0 / values.shape[0])


def norm(raw, cot, gain):
    centre = raw - mean0(raw)
    rstd = lax.rsqrt(mean0(centre * centre) + 1e-05)
    normed = centre * rstd
    dn = cot * gain
    grad = rstd * (dn - mean0(dn) - normed * mean0(dn * normed))
    return normed * gain, cot * normed, grad


def front_kernel(
    pieces,
    part_ref,
    wl_ref,
    emb_ref,
    up_ref,
    bias_ref,
    wl_out,
    emb_out,
    flat_ref,
    hidden_ref,
    pre_ref,
    cgot,
    cmine,
    cother,
    comp,
    compf,
    embf,
    part,
    got,
    mine,
    other,
    csems,
    wsems,
    esems,
    psems,
):
    at = Place()
    fields, width, examples = emb_ref.shape
    step, kk = width // 4, part_ref.shape[1]
    scale = float(width) ** (-0.5)
    block = embf.shape[0]
    size = fields // pieces
    background = []

    def piece(p):
        here = pl.ds(p * size, size)
        for k in (1, 2, 3):
            y, peer = at.to_y(k)
            background.append(
                send(emb_ref.at[here, rows(y, step), :], emb_out.at[k, here], esems, p * 3 + k - 1, peer)
            )

    def own_part():
        wl_out[0] = jnp.zeros(wl_out.shape[1:], BF16)
        wl_out[0, :, : wl_ref.shape[1]] = wl_ref[...]
        emb_out[0] = emb_ref[:, rows(at.y, step), :]

    greet(at.field_group(), own_part)
    copies = []
    for k in (1, 2, 3):
        y, peer = at.to_y(k)
        copies.append(send(part_ref.at[rows(y, step)], cgot.at[k - 1], csems, k - 1, peer))
    for k in (1, 2, 3):
        background.append(send(wl_out.at[0], wl_out.at[k], wsems, k - 1, at.to_y(k)[1]))
    for copy in copies:
        copy.wait()
    cmine[...] = (
        part_ref[rows(at.y, step)].astype(F32)
        + cgot[0].astype(F32)
        + cgot[1].astype(F32)
        + cgot[2].astype(F32)
    ).astype(BF16)
    copy = send(cmine, cother, csems, 3, at.to_zh()[1])
    piece(0)
    piece(1)
    copy.wait()
    own = rows(at.y, step)
    comp[own] = (cmine[...].astype(F32) + cother[...].astype(F32)).astype(BF16)
    copies = [send(comp.at[own], comp.at[own], csems, 3 + k, at.to_y(k)[1]) for k in (1, 2, 3)]
    for copy in copies:
        copy.wait()
    compf[...] = comp[...].astype(F32)

    def interact(start, stop):
        @pl.loop(start, stop)
        def _(i):
            embf[...] = emb_ref[pl.ds(i * block, block)].astype(F32)

            def terms(e, totals):
                c = compf[e]
                return tuple(t + c * embf[j, pl.ds(e, 1), :] for j, t in enumerate(totals))

            totals = lax.fori_loop(
                0, width, terms, tuple(jnp.zeros((kk, examples), F32) for _ in range(block)), unroll=8
            )
            for j in range(block):
                flat_ref[i * block + j] = (totals[j] * scale).astype(BF16)

    blocks = fields // block
    cuts = [blocks * p // 3 for p in range(4)]
    for p in range(3):
        piece(2 + p)
        interact(cuts[p], cuts[p + 1])

    flat = flat_ref[...].reshape(fields * kk, examples)
    units = up_ref.shape[0]
    quarter = units // 4

    @pl.loop(0, 4)
    def _(r):
        part[rows(r, quarter)] = jnp.dot(
            up_ref[rows(r, quarter), :], flat, preferred_element_type=F32
        ).astype(BF16)

    def after(p):
        def go():
            if p < pieces:
                piece(p)

        return go

    bias = jnp.transpose(jnp.broadcast_to(bias_ref[:, rows(at.y, quarter)], (examples, quarter)))
    pre = field_sum(at, part, got, mine, other, psems, after(5)) + bias
    pre_ref[...] = pre
    hidden_ref[rows(at.y, quarter)] = (pre / (1.0 + jnp.exp(-pre))).astype(BF16)
    for copy in gather_rows(at, hidden_ref, psems):
        copy.wait()
    for copy in background:
        copy.wait()


class BatchSum:
    def __init__(self, at, ref, one, two, three, sems, out):
        self.at, self.ref, self.one, self.two, self.three, self.sems, self.out = (
            at, ref, one, two, three, sems, out,
        )

    def first(self):
        core, peer = self.at.to_core()
        self.copies = [send(self.ref.at[:, core], self.one, self.sems, 0, peer)]

    def wait(self):
        for copy in self.copies:
            copy.wait()

    def second(self):
        self.wait()
        one = self.one

        @pl.loop(0, 16)
        def _(j):
            one[j] = (one[j].astype(F32) + self.ref[j, self.at.core].astype(F32)).astype(BF16)

        self.copies = []
        for k in (1, 2, 3):
            x, peer = self.at.to_x(k)
            self.copies.append(send(one.at[pl.ds(x * 4, 4)], self.two.at[k - 1], self.sems, k, peer))

    def third(self):
        self.wait()
        for j in range(4):
            total = self.one[self.at.x * 4 + j].astype(F32)
            for k in range(3):
                total = total + self.two[k, j].astype(F32)
            self.two[0, j] = total.astype(BF16)
        self.copies = []
        for k in (1, 2, 3):
            z, peer = self.at.to_zl(k)
            self.copies.append(send(self.two.at[0, z], self.three.at[k - 1], self.sems, 3 + k, peer))

    def last(self):
        self.wait()
        total = self.two[0, self.at.zl].astype(F32)
        for k in range(3):
            total = total + self.three[k].astype(F32)
        self.out[...] = total


def back_kernel(
    hidden_ref,
    pre_ref,
    down_ref,
    cot_ref,
    gain_ref,
    lin_ref,
    flat_ref,
    up_ref,
    emb_ref,
    lcot_ref,
    fm_ref,
    out_ref,
    gather_ref,
    gcomp_ref,
    down_out,
    up_out,
    rows_out,
    gfm_ref,
    gpre_ref,
    part,
    got,
    mine,
    other,
    lmine,
    lother,
    raw_ref,
    glc,
    dpart,
    upart,
    d1,
    d2,
    d3,
    u1,
    u2,
    u3,
    interf,
    embf,
    cb,
    cgot,
    cmine,
    cother,
    rsum,
    rmine,
    rgot,
    rtotal,
    rother,
    hsems,
    lsems,
    ysems,
    zsems,
    csems,
    dsems,
    usems,
    rsems,
):
    at = Place()
    units, examples = hidden_ref.shape
    fields, width = emb_ref.shape[:2]
    quarter, step, kk = units // 4, width // 4, flat_ref.shape[1]
    scale = float(width) ** (-0.5)
    chunk = raw_ref.shape[0]
    half = 4 * chunk
    zh, zpeer = at.to_zh()
    zbase = at.zh * half
    own = rows(at.y, step)
    gain = gain_ref[...]
    lcopies = []

    def linear(j):
        field = lax.rem(at.y + 1 + j, 4) * chunk
        lcopies.append(
            send(lin_ref.at[pl.ds(zh * half + field, chunk)], lother.at[pl.ds(field, chunk)], lsems, j, zpeer)
        )

    def column_sums(values):
        return jnp.sum(jnp.transpose(values), axis=0, keepdims=True)

    n_bias = units // rmine.shape[1]

    def forward():
        rmine[...] = jnp.zeros_like(rmine)
        hidden = jnp.transpose(hidden_ref[...].astype(F32)).astype(BF16)
        gain_total = jnp.zeros((width, examples), F32)
        for n in range(0, cot_ref.shape[0], 2):
            raw = jnp.transpose(
                jnp.dot(hidden, down_ref[:, n * width : (n + 2) * width], preferred_element_type=F32)
            )
            for m in range(2):
                out, term, grad = norm(
                    raw[m * width : (m + 1) * width], cot_ref[n + m].astype(F32), gain
                )
                fm_ref[n + m] = out.astype(BF16)
                gain_total = gain_total + term
                gfm_ref[n + m] = grad.astype(BF16)
        rsum[...] = gain_total

    greet(at.field_group() + at.batch_group(), forward)
    linear(0)
    linear(1)
    gfm = gfm_ref[...].reshape(down_ref.shape[1], examples)

    @pl.loop(0, 4)
    def _(r):
        part[rows(r, quarter)] = jnp.dot(
            down_ref[rows(r, quarter), :], gfm, preferred_element_type=F32
        ).astype(BF16)

    copies = []
    for k in (1, 2, 3):
        y, peer = at.to_y(k)
        copies.append(send(part.at[rows(y, quarter)], got.at[k - 1], hsems, k - 1, peer))

    def weights(left_ref, right, into):
        @pl.loop(0, 4)
        def _(r):
            block = lax.dot_general(
                left_ref[rows(r, quarter), :],
                right,
                (((1,), (1,)), ((), ())),
                preferred_element_type=F32,
            ).astype(BF16)
            into[rows(r, 4)] = block.reshape((4,) + into.shape[1:])

    weights(hidden_ref, gfm, dpart)
    down = BatchSum(at, dpart, d1, d2, d3, dsems, down_out)
    down.first()
    for copy in copies:
        copy.wait()
    mine[...] = (
        part[rows(at.y, quarter)].astype(F32)
        + got[0].astype(F32)
        + got[1].astype(F32)
        + got[2].astype(F32)
    ).astype(BF16)
    copy = send(mine, other, hsems, 3, zpeer)
    linear(2)
    linear(3)
    down.second()
    pre = pre_ref[...]
    sigma = 1.0 / (1.0 + jnp.exp(-pre))
    slope = sigma * (1.0 + pre * (1.0 - sigma))
    copy.wait()
    grad = (mine[...].astype(F32) + other[...].astype(F32)) * slope
    gpre_ref[rows(at.y, quarter)] = grad.astype(BF16)
    copies = gather_rows(at, gpre_ref, hsems)
    rmine[pl.ds(at.y, 1), :] = 0.5 * column_sums(grad)
    ycopies = []

    def linear_sum(j):
        lcopies[j].wait()
        field, peer = at.to_y(j + 1)
        for n in range(chunk):
            lmine[field * chunk + n] = (
                lin_ref[zbase + field * chunk + n].astype(F32) + lother[field * chunk + n].astype(F32)
            ).astype(BF16)
        if j < 3:
            ycopies.append(
                send(lmine.at[pl.ds(field * chunk, chunk)], raw_ref.at[:, own, :], lsems, 4 + j, peer)
            )

    linear_sum(0)
    for copy in copies:
        copy.wait()
    flat = flat_ref[...].reshape(fields * kk, examples)
    gpre = gpre_ref[...]
    weights(gpre_ref, flat, upart)
    up = BatchSum(at, upart, u1, u2, u3, usems, up_out)
    up.first()
    linear_sum(1)

    @pl.loop(0, 6)
    def _(r):
        size = fields * kk // 6
        block = lax.dot_general(
            up_ref[:, rows(r, size)], gpre, (((0,), (0,)), ((), ())), preferred_element_type=F32
        ).astype(BF16)
        interf[rows(r, fields // 6)] = block.astype(F32).reshape(fields // 6, kk, examples)

    linear_sum(2)
    down.third()
    block = embf.shape[1]

    def compression(start, stop):
        @pl.loop(start, stop)
        def _(i):
            embf[...] = emb_ref[:, rows(i, block), :].astype(F32)

            def terms(f, totals):
                g = interf[f]
                return tuple(t + g * embf[f, pl.ds(j, 1), :] for j, t in enumerate(totals))

            totals = lax.fori_loop(
                0, fields, terms, tuple(jnp.zeros((kk, examples), F32) for _ in range(block)), unroll=4
            )
            for j in range(block):
                cb[i * block + j] = totals[j].astype(BF16)

    blocks = width // block
    up.second()
    linear_sum(3)
    raw_ref[:, own, :] = lmine[pl.ds(at.y * chunk, chunk)]
    compression(0, blocks // 3)
    for copy in ycopies:
        copy.wait()

    @pl.loop(0, chunk)
    def _(n):
        out, term, grad = norm(raw_ref[n].astype(F32), lcot_ref[n].astype(F32), gain)
        out_ref[n] = out.astype(BF16)
        rsum[...] += term
        glc[n] = grad.astype(BF16)

    mid = pl.ds(zbase + at.y * chunk, chunk)
    gather_ref[mid] = glc[:, own, :]
    zcopies = [send(gather_ref.at[mid], gather_ref.at[mid], zsems, 0, zpeer)]
    gcopies = []
    for k in (1, 2, 3):
        y, peer = at.to_y(k)
        gcopies.append(send(glc.at[:, rows(y, step), :], gather_ref.at[mid], ysems, k - 1, peer))
    rmine[n_bias : n_bias + 1, :width] = column_sums(rsum[...])
    rcopies = [send(rmine, rgot.at[k - 1], rsems, k - 1, at.to_y(k)[1]) for k in (1, 2, 3)]
    compression(blocks // 3, 2 * blocks // 3)
    for k in (1, 2, 3):
        gcopies[k - 1].wait()
        source = lax.rem(at.y + 4 - k, 4)
        there = pl.ds(zbase + source * chunk, chunk)
        zcopies.append(send(gather_ref.at[there], gather_ref.at[there], zsems, k, zpeer))
    for copy in rcopies:
        copy.wait()
    rtotal[...] = (rmine[...] + rgot[1]) + (rgot[0] + rgot[2])
    rcopy = send(rtotal, rother, rsems, 3, zpeer)
    compression(2 * blocks // 3, blocks)
    ccopies = []
    for k in (1, 2, 3):
        y, peer = at.to_y(k)
        ccopies.append(send(cb.at[rows(y, step)], cgot.at[k - 1], csems, k - 1, peer))
    down.last()
    for copy in ccopies:
        copy.wait()
    cmine[...] = (
        cb[own].astype(F32) + cgot[0].astype(F32) + cgot[1].astype(F32) + cgot[2].astype(F32)
    ).astype(BF16)
    ccopy = send(cmine, cother, csems, 3, zpeer)
    up.third()
    rcopy.wait()
    rows_out[...] = rtotal[...] + rother[...]
    ccopy.wait()
    gcomp_ref[...] = ((cmine[...].astype(F32) + cother[...].astype(F32)) * scale).astype(BF16)
    up.last()
    for copy in zcopies:
        copy.wait()


def small_kernel(
    nl, part_ref, rows_ref, lin_ref, comp_ref, rows_out, psend, ygot, one, xmine, xgot, zmine, zgot, sems
):
    at = Place()
    fields, kk = lin_ref.shape[0], comp_ref.shape[0]
    psend[...] = part_ref[...].astype(BF16)
    greet(at.y_group() + at.batch_group())
    copies = []
    for k in (1, 2, 3):
        copies.append(send(psend.at[k], ygot.at[k - 1], sems, k - 1, at.to_y(4 - k)[1]))
    half = rows_ref.shape[0]
    one[0, fields : fields + half] = rows_ref[:, :128]
    one[0, fields + half :] = rows_ref[:, 128:]
    for copy in copies:
        copy.wait()
    one[0, :fields] = (
        part_ref[0] + ygot[0].astype(F32) + ygot[1].astype(F32) + ygot[2].astype(F32)
    )
    send(one.at[0], one.at[1], sems, 3, at.to_core()[1]).wait()
    xmine[...] = (one[0] + one[1]).astype(BF16)
    copies = [send(xmine, xgot.at[k - 1], sems, 3 + k, at.to_x(k)[1]) for k in (1, 2, 3)]
    for copy in copies:
        copy.wait()
    zmine[...] = (
        (xmine[...].astype(F32) + xgot[1].astype(F32))
        + (xgot[0].astype(F32) + xgot[2].astype(F32))
    ).astype(BF16)
    copies = [send(zmine, zgot.at[k - 1], sems, 6 + k, at.to_zl(k)[1]) for k in (1, 2, 3)]
    for copy in copies:
        copy.wait()
    total = (zmine[...].astype(F32) + zgot[1].astype(F32)) + (
        zgot[0].astype(F32) + zgot[2].astype(F32)
    )
    lin_ref[...] = total[:fields, :nl]
    comp_ref[...] = jnp.transpose(total[:fields])[nl : nl + kk]
    rows_out[:, :128] = total[fields : fields + half]
    rows_out[:, 128:] = total[fields + half :]


def local(embeddings, compress, w_up, up_bias, w_down, w_linear, ln_gain, cot_fm, cot_lc):
    examples, fields, width = embeddings.shape
    units, kk, nl = w_up.shape[0], compress.shape[1], w_linear.shape[1]
    part, quarter, own_rows = width // 4, units // 4, units // 32
    turned = embeddings.transpose(1, 2, 0)
    gain = jnp.broadcast_to(ln_gain.reshape(-1, 1), (width, examples))
    comp_part = jnp.einsum("feb,fk->ekb", turned, compress, preferred_element_type=F32).astype(BF16)
    cot_first, cot_second = cot_fm.transpose(1, 2, 0), cot_lc.transpose(1, 2, 0)
    pieces, block = 6, 8

    def stages(columns):
        return [
            VMEM((16, own_rows, columns), BF16),
            VMEM((3, 4, own_rows, columns), BF16),
            VMEM((3, own_rows, columns), BF16),
        ]

    row_scratch = [
        VMEM((units, examples), BF16),
        VMEM((3, quarter, examples), BF16),
        VMEM((quarter, examples), BF16),
        VMEM((quarter, examples), BF16),
    ]
    wl_all, spread, flat, hidden, hidden_pre = call(
        functools.partial(front_kernel, pieces),
        [
            ((4, fields, 128), BF16),
            ((4, fields, part, examples), BF16),
            ((fields, kk, examples), BF16),
            ((units, examples), BF16),
            ((quarter, examples), F32),
        ],
        [
            VMEM((3, part, kk, examples), BF16),
            VMEM((part, kk, examples), BF16),
            VMEM((part, kk, examples), BF16),
            VMEM((width, kk, examples), BF16),
            VMEM((width, kk, examples), F32),
            VMEM((block, width, examples), F32),
        ]
        + row_scratch
        + [
            pltpu.SemaphoreType.DMA((2, 7)),
            pltpu.SemaphoreType.DMA((2, 3)),
            pltpu.SemaphoreType.DMA((2, 3 * pieces)),
            pltpu.SemaphoreType.DMA((2, 7)),
        ],
        0,
        80,
        16,
        comp_part,
        w_linear,
        turned,
        w_up,
        up_bias.reshape(1, -1),
    )
    spread = spread.reshape(4 * fields, part, examples)
    lin = jnp.einsum(
        "feb,fn->neb", spread, wl_all.reshape(4 * fields, 128)[:, :nl], preferred_element_type=F32
    ).astype(BF16)
    columns = cot_first.shape[0] * width
    extra_shape = (8, 256)
    n_bias, n_extra, slab = units // 256, 8, 16
    fm_out, lc_out, gathered, grad_comp, grad_down, grad_up, extra = call(
        back_kernel,
        [
            (cot_first.shape, BF16),
            (cot_second.shape, BF16),
            ((nl, part, examples), BF16),
            ((part, kk, examples), BF16),
            ((own_rows, columns), F32),
            ((own_rows, fields * kk), F32),
            (extra_shape, F32),
        ],
        [VMEM(cot_first.shape, BF16), VMEM((units, examples), BF16)]
        + row_scratch
        + [
            VMEM((nl // 2, part, examples), BF16),
            VMEM((nl // 2, part, examples), BF16),
            VMEM(cot_second.shape, BF16),
            VMEM(cot_second.shape, BF16),
            VMEM((16, 2, own_rows, columns), BF16),
            VMEM((16, 2, own_rows, fields * kk), BF16),
        ]
        + stages(columns)
        + stages(fields * kk)
        + [
            VMEM((fields, kk, examples), F32),
            VMEM((fields, slab, examples), F32),
            VMEM((width, kk, examples), BF16),
            VMEM((3, part, kk, examples), BF16),
            VMEM((part, kk, examples), BF16),
            VMEM((part, kk, examples), BF16),
            VMEM((width, examples), F32),
            VMEM(extra_shape, F32),
            VMEM((3,) + extra_shape, F32),
            VMEM(extra_shape, F32),
            VMEM(extra_shape, F32),
            pltpu.SemaphoreType.DMA((2, 7)),
            pltpu.SemaphoreType.DMA((2, 7)),
            pltpu.SemaphoreType.DMA((2, 3)),
            pltpu.SemaphoreType.DMA((2, 4)),
            pltpu.SemaphoreType.DMA((2, 4)),
            pltpu.SemaphoreType.DMA((2, 7)),
            pltpu.SemaphoreType.DMA((2, 7)),
            pltpu.SemaphoreType.DMA((2, 4)),
        ],
        1,
        80,
        28,
        hidden,
        hidden_pre,
        w_down,
        cot_first,
        gain,
        lin,
        flat,
        w_up,
        turned,
        cot_second,
    )
    mixed = jnp.concatenate(
        [
            jnp.einsum("feb,neb->fn", spread, gathered, preferred_element_type=F32),
            jnp.einsum("feb,ekb->fk", spread, grad_comp, preferred_element_type=F32),
            jnp.zeros((4 * fields, 128 - nl - kk), F32),
        ],
        axis=1,
    ).reshape(4, fields, 128)
    total_rows = fields + 2 * n_extra
    grad_linear, grad_compress, extra = call(
        functools.partial(small_kernel, nl),
        [((fields, nl), F32), ((kk, fields), F32), (extra.shape, F32)],
        [
            VMEM((4, fields, 128), BF16),
            VMEM((3, fields, 128), BF16),
            VMEM((2, total_rows, 128), F32),
            VMEM((total_rows, 128), BF16),
            VMEM((3, total_rows, 128), BF16),
            VMEM((total_rows, 128), BF16),
            VMEM((3, total_rows, 128), BF16),
            pltpu.SemaphoreType.DMA((2, 10)),
        ],
        2,
        15,
        8,
        mixed,
        extra,
    )
    grad_bias = extra[:n_bias].reshape(-1)
    grad_gain = extra[n_bias, :width]
    return (
        fm_out.transpose(2, 0, 1),
        lc_out.transpose(2, 0, 1),
        grad_compress.T,
        grad_up,
        grad_bias,
        grad_down,
        grad_linear,
        grad_gain,
    )


def solution(mesh):
    placed = (
        P("batch", "field", None),
        P("field", None),
        P(None, "field"),
        P(),
        P(None, "field"),
        P("field", None),
        P(),
        P("batch", "field", None),
        P("batch", "field", None),
    )
    return jax.shard_map(
        local,
        mesh=mesh,
        in_specs=placed,
        out_specs=(
            P("batch", "field", None),
            P("batch", "field", None),
            P("field", None),
            P("batch", "field"),
            P(),
            P("batch", "field"),
            P("field", None),
            P(),
        ),
        check_vma=False,
    )
```

```python
import functools

import jax
import jax.numpy as jnp
from jax import lax
from jax.experimental import pallas as pl
from jax.experimental.pallas import tpu as pltpu
from jax.sharding import PartitionSpec as P

MESH = pl.DeviceIdType.MESH
VMEM = pltpu.VMEM
F32 = jnp.float32
BF16 = jnp.bfloat16
MIB = 1024 * 1024


class Place:
    def __init__(self):
        batch, field = lax.axis_index("batch"), lax.axis_index("field")
        self.batch, self.field = batch, field
        self.y, self.zh = lax.rem(field, 4), lax.div(field, 4)
        self.core = lax.rem(batch, 2)
        self.zl = lax.rem(lax.div(batch, 2), 4)
        self.x = lax.div(batch, 8)

    def to_y(self, k):
        other = lax.rem(self.y + k, 4)
        return other, (self.batch, self.zh * 4 + other)

    def to_zh(self):
        other = 1 - self.zh
        return other, (self.batch, other * 4 + self.y)

    def to_core(self):
        other = 1 - self.core
        return other, (self.x * 8 + self.zl * 2 + other, self.field)

    def to_x(self, k):
        other = lax.rem(self.x + k, 4)
        return other, (other * 8 + self.zl * 2 + self.core, self.field)

    def to_zl(self, k):
        other = lax.rem(self.zl + k, 4)
        return other, (self.x * 8 + other * 2 + self.core, self.field)

    def y_group(self):
        return [self.to_y(k)[1] for k in (1, 2, 3)]

    def field_group(self):
        return self.y_group() + [self.to_zh()[1]]

    def batch_group(self):
        return [self.to_core()[1]] + [self.to_x(k)[1] for k in (1, 2, 3)] + [self.to_zl(k)[1] for k in (1, 2, 3)]


def greet(peers, work=None):
    barrier = pltpu.get_barrier_semaphore()
    for peer in peers:
        pl.semaphore_signal(barrier, inc=1, device_id=peer, device_id_type=MESH)
    if work is not None:
        work()
    pl.semaphore_wait(barrier, len(peers))


def send(src, dst, sems, index, peer):
    copy = pltpu.make_async_remote_copy(
        src_ref=src,
        dst_ref=dst,
        send_sem=sems.at[0, index],
        recv_sem=sems.at[1, index],
        device_id=peer,
        device_id_type=MESH,
    )
    copy.start()
    return copy


def params(collective_id, mib):
    return pltpu.CompilerParams(
        collective_id=collective_id, has_side_effects=True, vmem_limit_bytes=mib * MIB
    )


def cost(us):
    return pl.CostEstimate(flops=0, bytes_accessed=int(us * 3.0e6), transcendentals=0)


def call(kernel, outs, scratch, collective_id, us, mib, *args):
    return pl.pallas_call(
        kernel,
        out_shape=[jax.ShapeDtypeStruct(shape, dtype) for shape, dtype in outs],
        in_specs=[pl.BlockSpec(memory_space=VMEM)] * len(args),
        out_specs=[pl.BlockSpec(memory_space=VMEM)] * len(outs),
        scratch_shapes=scratch,
        compiler_params=params(collective_id, mib),
        cost_estimate=cost(us),
    )(*args)


def rows(start, size):
    return pl.ds(pl.multiple_of(start * size, size), size)


def gather_rows(at, out_ref, sems):
    own = rows(at.y, out_ref.shape[0] // 4)
    return [send(out_ref.at[own], out_ref.at[own], sems, 3 + k, at.to_y(k)[1]) for k in (1, 2, 3)]


def mean0(values):
    return jnp.sum(values, axis=0, keepdims=True) * (1.0 / values.shape[0])


def norm(raw, cot, gain):
    centre = raw - mean0(raw)
    rstd = lax.rsqrt(mean0(centre * centre) + 1e-05)
    normed = centre * rstd
    dn = cot * gain
    grad = rstd * (dn - mean0(dn) - normed * mean0(dn * normed))
    return normed * gain, cot * normed, grad


class BatchSum:
    def __init__(self, at, ref, one, two, three, sems, out):
        self.at, self.ref, self.one, self.two, self.three, self.sems, self.out = (
            at, ref, one, two, three, sems, out,
        )

    def first(self):
        core, peer = self.at.to_core()
        self.copies = [send(self.ref.at[:, core], self.one, self.sems, 0, peer)]

    def wait(self):
        for copy in self.copies:
            copy.wait()

    def second(self):
        self.wait()
        one = self.one

        @pl.loop(0, 16)
        def _(j):
            one[j] = (one[j].astype(F32) + self.ref[j, self.at.core].astype(F32)).astype(BF16)

        self.copies = []
        for k in (1, 2, 3):
            x, peer = self.at.to_x(k)
            self.copies.append(send(one.at[pl.ds(x * 4, 4)], self.two.at[k - 1], self.sems, k, peer))

    def third(self):
        self.wait()
        for j in range(4):
            total = self.one[self.at.x * 4 + j].astype(F32)
            for k in range(3):
                total = total + self.two[k, j].astype(F32)
            self.two[0, j] = total.astype(BF16)
        self.copies = []
        for k in (1, 2, 3):
            z, peer = self.at.to_zl(k)
            self.copies.append(send(self.two.at[0, z], self.three.at[k - 1], self.sems, 3 + k, peer))

    def last(self):
        self.wait()
        total = self.two[0, self.at.zl].astype(F32)
        for k in range(3):
            total = total + self.three[k].astype(F32)
        self.out[...] = total


def layer_kernel(
    pieces,
    part_ref,
    wl_ref,
    emb_ref,
    up_ref,
    bias_ref,
    down_ref,
    cot_ref,
    gain_ref,
    lcot_ref,
    emb_out,
    fm_ref,
    out_ref,
    gather_ref,
    gcomp_ref,
    down_out,
    up_out,
    rows_out,
    wl_out,
    flat_ref,
    hidden_ref,
    pre_ref,
    comp,
    compf,
    ccgot,
    ccmine,
    ccother,
    embi,
    embx,
    linf,
    lin_ref,
    part,
    got,
    mine,
    other,
    gfm_ref,
    gpre_ref,
    hpart,
    hgot,
    hmine,
    hother,
    lmine,
    lother,
    raw_ref,
    glc,
    dpart,
    upart,
    d1,
    d2,
    d3,
    u1,
    u2,
    u3,
    interf,
    embf,
    cb,
    cgot,
    cmine,
    cother,
    rsum,
    rmine,
    rgot,
    rtotal,
    rother,
    ccsems,
    wsems,
    esems,
    psems,
    hsems,
    lsems,
    ysems,
    zsems,
    csems,
    dsems,
    usems,
    rsems,
):
    at = Place()
    fields, width, examples = emb_ref.shape
    step, kk = width // 4, part_ref.shape[1]
    scale = float(width) ** (-0.5)
    block = embi.shape[0]
    slab = embx.shape[0] // (4 * fields)
    background = []
    moved = []

    def piece(p):
        here = pl.ds(p % 2 * (fields // 2), fields // 2)
        for k in (1, 2, 3):
            y, peer = at.to_y(k)
            there = pl.ds(pl.multiple_of(y * step + p // 2 * slab, slab), slab)
            moved.append(
                send(
                    emb_ref.at[here, there, :],
                    emb_out.at[k, here, pl.ds(p // 2 * slab, slab), :],
                    esems,
                    p * 3 + k - 1,
                    peer,
                )
            )

    def own_part():
        wl_out[0] = jnp.zeros(wl_out.shape[1:], BF16)
        wl_out[0, :, : wl_ref.shape[1]] = wl_ref[...]
        emb_out[0] = emb_ref[:, rows(at.y, step), :]

    greet(at.field_group() + at.batch_group(), own_part)
    copies = []
    for k in (1, 2, 3):
        y, peer = at.to_y(k)
        copies.append(send(part_ref.at[rows(y, step)], ccgot.at[k - 1], ccsems, k - 1, peer))
    for k in (1, 2, 3):
        background.append(send(wl_out.at[0], wl_out.at[k], wsems, k - 1, at.to_y(k)[1]))
    for copy in copies:
        copy.wait()
    ccmine[...] = (
        part_ref[rows(at.y, step)].astype(F32)
        + ccgot[0].astype(F32)
        + ccgot[1].astype(F32)
        + ccgot[2].astype(F32)
    ).astype(BF16)
    copy = send(ccmine, ccother, ccsems, 3, at.to_zh()[1])
    piece(0)
    piece(1)
    copy.wait()
    own = rows(at.y, step)
    comp[own] = (ccmine[...].astype(F32) + ccother[...].astype(F32)).astype(BF16)
    copies = [send(comp.at[own], comp.at[own], ccsems, 3 + k, at.to_y(k)[1]) for k in (1, 2, 3)]
    for copy in copies:
        copy.wait()
    compf[...] = comp[...].astype(F32)

    def interact(start, stop):
        @pl.loop(start, stop)
        def _(i):
            embi[...] = emb_ref[pl.ds(i * block, block)].astype(F32)

            def terms(e, totals):
                c = compf[e]
                return tuple(t + c * embi[j, pl.ds(e, 1), :] for j, t in enumerate(totals))

            totals = lax.fori_loop(
                0, width, terms, tuple(jnp.zeros((kk, examples), F32) for _ in range(block)), unroll=8
            )
            for j in range(block):
                flat_ref[i * block + j] = (totals[j] * scale).astype(BF16)

    blocks = fields // block
    cuts = [blocks * p // 3 for p in range(4)]
    for p in range(3):
        if p < 2:
            piece(2 + p)
        interact(cuts[p], cuts[p + 1])

    flat = flat_ref[...].reshape(fields * kk, examples)
    units = up_ref.shape[0]
    quarter = units // 4

    @pl.loop(0, 4)
    def _(r):
        part[rows(r, quarter)] = jnp.dot(
            up_ref[rows(r, quarter), :], flat, preferred_element_type=F32
        ).astype(BF16)

    bias = jnp.transpose(jnp.broadcast_to(bias_ref[:, rows(at.y, quarter)], (examples, quarter)))
    copies = []
    for k in (1, 2, 3):
        y, peer = at.to_y(k)
        copies.append(send(part.at[rows(y, quarter)], got.at[k - 1], psems, k - 1, peer))

    for copy in background:
        copy.wait()
    wt = jnp.transpose(wl_out[...].reshape(4 * fields, wl_out.shape[2]).astype(F32))
    wt = wt[: lin_ref.shape[0]].astype(BF16)
    n_lin = lin_ref.shape[0]
    zh, zpeer = at.to_zh()
    lcopies = []

    def linear(g):
        for copy in moved[6 * g : 6 * g + 6]:
            copy.wait()
        for k in range(4):

            @pl.loop(0, fields // 8)
            def _(i):
                embx[rows(k * (fields // 8) + i, 8 * slab), :] = (
                    emb_out[k, pl.ds(i * 8, 8), g * slab : (g + 1) * slab, :]
                    .astype(F32)
                    .reshape(8 * slab, examples)
                )

        for e in range(slab):
            linf[pl.ds(e, n_lin, stride=slab), :] = jnp.dot(
                wt,
                embx[pl.ds(e, 4 * fields, stride=slab), :].astype(BF16),
                preferred_element_type=F32,
            )
        here = slice(g * slab, (g + 1) * slab)
        lin_ref[:, here, :] = linf[...].reshape(n_lin, slab, examples).astype(BF16)
        lcopies.append(
            send(
                lin_ref.at[pl.ds(zh * (n_lin // 2), n_lin // 2), here, :],
                lother.at[:, here, :],
                lsems,
                g,
                zpeer,
            )
        )

    linear(0)
    for copy in copies:
        copy.wait()
    mine[...] = (
        part[rows(at.y, quarter)].astype(F32)
        + got[0].astype(F32)
        + got[1].astype(F32)
        + got[2].astype(F32)
    ).astype(BF16)
    copy = send(mine, other, psems, 3, zpeer)
    piece(4)
    linear(1)
    copy.wait()
    pre = mine[...].astype(F32) + other[...].astype(F32) + bias
    pre_ref[...] = pre
    hidden_ref[rows(at.y, quarter)] = (pre / (1.0 + jnp.exp(-pre))).astype(BF16)
    for copy in gather_rows(at, hidden_ref, psems):
        copy.wait()
    chunk = raw_ref.shape[0]
    half = 4 * chunk
    zbase = at.zh * half
    own = rows(at.y, step)
    gain = gain_ref[...]
    ycopies = []

    def linear_sum(g):
        lcopies[g].wait()
        here = slice(g * slab, (g + 1) * slab)
        there = pl.ds(pl.multiple_of(at.y * step + g * slab, slab), slab)
        lmine[:, here, :] = (
            lin_ref[pl.ds(zbase, half), here, :].astype(F32) + lother[:, here, :].astype(F32)
        ).astype(BF16)
        for k in (1, 2, 3):
            y, peer = at.to_y(k)
            ycopies.append(
                send(
                    lmine.at[pl.ds(y * chunk, chunk), here, :],
                    raw_ref.at[:, there, :],
                    lsems,
                    3 + g * 3 + k - 1,
                    peer,
                )
            )
        raw_ref[:, there, :] = lmine[pl.ds(at.y * chunk, chunk), here, :]

    def column_sums(values):
        return jnp.sum(jnp.transpose(values), axis=0, keepdims=True)

    n_bias = units // rmine.shape[1]

    def forward():
        rmine[...] = jnp.zeros_like(rmine)
        hidden = jnp.transpose(hidden_ref[...].astype(F32)).astype(BF16)
        gain_total = jnp.zeros((width, examples), F32)
        for n in range(0, cot_ref.shape[0], 2):
            raw = jnp.transpose(
                jnp.dot(hidden, down_ref[:, n * width : (n + 2) * width], preferred_element_type=F32)
            )
            for m in range(2):
                out, term, grad = norm(
                    raw[m * width : (m + 1) * width], cot_ref[n + m].astype(F32), gain
                )
                fm_ref[n + m] = out.astype(BF16)
                gain_total = gain_total + term
                gfm_ref[n + m] = grad.astype(BF16)
        rsum[...] = gain_total

    piece(5)
    linear_sum(0)
    forward()
    gfm = gfm_ref[...].reshape(down_ref.shape[1], examples)

    @pl.loop(0, 4)
    def _(r):
        hpart[rows(r, quarter)] = jnp.dot(
            down_ref[rows(r, quarter), :], gfm, preferred_element_type=F32
        ).astype(BF16)

    copies = []
    for k in (1, 2, 3):
        y, peer = at.to_y(k)
        copies.append(send(hpart.at[rows(y, quarter)], hgot.at[k - 1], hsems, k - 1, peer))

    def weights(left_ref, right, into):
        @pl.loop(0, 4)
        def _(r):
            block = lax.dot_general(
                left_ref[rows(r, quarter), :],
                right,
                (((1,), (1,)), ((), ())),
                preferred_element_type=F32,
            ).astype(BF16)
            into[rows(r, 4)] = block.reshape((4,) + into.shape[1:])

    weights(hidden_ref, gfm, dpart)
    down = BatchSum(at, dpart, d1, d2, d3, dsems, down_out)
    down.first()
    linear_sum(1)
    for copy in copies:
        copy.wait()
    hmine[...] = (
        hpart[rows(at.y, quarter)].astype(F32)
        + hgot[0].astype(F32)
        + hgot[1].astype(F32)
        + hgot[2].astype(F32)
    ).astype(BF16)
    copy = send(hmine, hother, hsems, 3, zpeer)
    linear(2)
    down.second()
    pre = pre_ref[...]
    sigma = 1.0 / (1.0 + jnp.exp(-pre))
    slope = sigma * (1.0 + pre * (1.0 - sigma))
    copy.wait()
    grad = (hmine[...].astype(F32) + hother[...].astype(F32)) * slope
    gpre_ref[rows(at.y, quarter)] = grad.astype(BF16)
    copies = gather_rows(at, gpre_ref, hsems)
    rmine[pl.ds(at.y, 1), :] = 0.5 * column_sums(grad)
    linear_sum(2)
    for copy in copies:
        copy.wait()
    flat = flat_ref[...].reshape(fields * kk, examples)
    gpre = gpre_ref[...]
    weights(gpre_ref, flat, upart)
    up = BatchSum(at, upart, u1, u2, u3, usems, up_out)
    up.first()

    block = embf.shape[1]

    def compression(start, stop):
        @pl.loop(start, stop)
        def _(i):
            embf[...] = emb_ref[:, rows(i, block), :].astype(F32)

            def terms(f, totals):
                g = interf[f]
                return tuple(t + g * embf[f, pl.ds(j, 1), :] for j, t in enumerate(totals))

            totals = lax.fori_loop(
                0, fields, terms, tuple(jnp.zeros((kk, examples), F32) for _ in range(block)), unroll=4
            )
            for j in range(block):
                cb[i * block + j] = totals[j].astype(BF16)

    blocks = width // block
    for copy in ycopies:
        copy.wait()

    @pl.loop(0, chunk)
    def _(n):
        out, term, grad = norm(raw_ref[n].astype(F32), lcot_ref[n].astype(F32), gain)
        out_ref[n] = out.astype(BF16)
        rsum[...] += term
        glc[n] = grad.astype(BF16)

    mid = pl.ds(zbase + at.y * chunk, chunk)
    gather_ref[mid] = glc[:, own, :]
    zcopies = [send(gather_ref.at[mid], gather_ref.at[mid], zsems, 0, zpeer)]
    gcopies = []
    for k in (1, 2, 3):
        y, peer = at.to_y(k)
        gcopies.append(send(glc.at[:, rows(y, step), :], gather_ref.at[mid], ysems, k - 1, peer))
    rmine[n_bias : n_bias + 1, :width] = column_sums(rsum[...])
    rcopies = [send(rmine, rgot.at[k - 1], rsems, k - 1, at.to_y(k)[1]) for k in (1, 2, 3)]
    @pl.loop(0, 6)
    def _(r):
        size = fields * kk // 6
        block = lax.dot_general(
            up_ref[:, rows(r, size)], gpre, (((0,), (0,)), ((), ())), preferred_element_type=F32
        ).astype(BF16)
        interf[rows(r, fields // 6)] = block.astype(F32).reshape(fields // 6, kk, examples)

    up.second()
    down.third()
    compression(0, blocks // 3)
    for k in (1, 2, 3):
        gcopies[k - 1].wait()
        source = lax.rem(at.y + 4 - k, 4)
        there = pl.ds(zbase + source * chunk, chunk)
        zcopies.append(send(gather_ref.at[there], gather_ref.at[there], zsems, k, zpeer))
    for copy in rcopies:
        copy.wait()
    rtotal[...] = (rmine[...] + rgot[1]) + (rgot[0] + rgot[2])
    rcopy = send(rtotal, rother, rsems, 3, zpeer)
    compression(blocks // 3, blocks)
    ccopies = []
    for k in (1, 2, 3):
        y, peer = at.to_y(k)
        ccopies.append(send(cb.at[rows(y, step)], cgot.at[k - 1], csems, k - 1, peer))
    up.third()
    for copy in ccopies:
        copy.wait()
    cmine[...] = (
        cb[own].astype(F32) + cgot[0].astype(F32) + cgot[1].astype(F32) + cgot[2].astype(F32)
    ).astype(BF16)
    ccopy = send(cmine, cother, csems, 3, zpeer)
    down.last()
    rcopy.wait()
    rows_out[...] = rtotal[...] + rother[...]
    ccopy.wait()
    gcomp_ref[...] = ((cmine[...].astype(F32) + cother[...].astype(F32)) * scale).astype(BF16)
    up.last()
    for copy in zcopies:
        copy.wait()


def small_kernel(
    nl, part_ref, rows_ref, lin_ref, comp_ref, rows_out, psend, ygot, one, xmine, xgot, zmine, zgot, sems
):
    at = Place()
    fields, kk = lin_ref.shape[0], comp_ref.shape[0]
    psend[...] = part_ref[...].astype(BF16)
    greet(at.y_group() + at.batch_group())
    copies = []
    for k in (1, 2, 3):
        copies.append(send(psend.at[k], ygot.at[k - 1], sems, k - 1, at.to_y(4 - k)[1]))
    half = rows_ref.shape[0]
    one[0, fields : fields + half] = rows_ref[:, :128]
    one[0, fields + half :] = rows_ref[:, 128:]
    for copy in copies:
        copy.wait()
    one[0, :fields] = (
        part_ref[0] + ygot[0].astype(F32) + ygot[1].astype(F32) + ygot[2].astype(F32)
    )
    send(one.at[0], one.at[1], sems, 3, at.to_core()[1]).wait()
    xmine[...] = (one[0] + one[1]).astype(BF16)
    copies = [send(xmine, xgot.at[k - 1], sems, 3 + k, at.to_x(k)[1]) for k in (1, 2, 3)]
    for copy in copies:
        copy.wait()
    zmine[...] = (
        (xmine[...].astype(F32) + xgot[1].astype(F32))
        + (xgot[0].astype(F32) + xgot[2].astype(F32))
    ).astype(BF16)
    copies = [send(zmine, zgot.at[k - 1], sems, 6 + k, at.to_zl(k)[1]) for k in (1, 2, 3)]
    for copy in copies:
        copy.wait()
    total = (zmine[...].astype(F32) + zgot[1].astype(F32)) + (
        zgot[0].astype(F32) + zgot[2].astype(F32)
    )
    lin_ref[...] = total[:fields, :nl]
    comp_ref[...] = jnp.transpose(total[:fields])[nl : nl + kk]
    rows_out[:, :128] = total[fields : fields + half]
    rows_out[:, 128:] = total[fields + half :]


def local(embeddings, compress, w_up, up_bias, w_down, w_linear, ln_gain, cot_fm, cot_lc):
    examples, fields, width = embeddings.shape
    units, kk, nl = w_up.shape[0], compress.shape[1], w_linear.shape[1]
    part, quarter, own_rows = width // 4, units // 4, units // 32
    turned = embeddings.transpose(1, 2, 0)
    gain = jnp.broadcast_to(ln_gain.reshape(-1, 1), (width, examples))
    comp_part = jnp.einsum("feb,fk->ekb", turned, compress, preferred_element_type=F32).astype(BF16)
    cot_first, cot_second = cot_fm.transpose(1, 2, 0), cot_lc.transpose(1, 2, 0)
    pieces, block = 6, 8

    def stages(columns):
        return [
            VMEM((16, own_rows, columns), BF16),
            VMEM((3, 4, own_rows, columns), BF16),
            VMEM((3, own_rows, columns), BF16),
        ]

    row_scratch = [
        VMEM((units, examples), BF16),
        VMEM((3, quarter, examples), BF16),
        VMEM((quarter, examples), BF16),
        VMEM((quarter, examples), BF16),
    ]
    columns = cot_first.shape[0] * width
    extra_shape = (8, 256)
    n_bias, n_extra, slab = units // 256, 8, 16
    spread, fm_out, lc_out, gathered, grad_comp, grad_down, grad_up, extra = call(
        functools.partial(layer_kernel, pieces),
        [
            ((4, fields, part, examples), BF16),
            (cot_first.shape, BF16),
            (cot_second.shape, BF16),
            ((nl, part, examples), BF16),
            ((part, kk, examples), BF16),
            ((own_rows, columns), F32),
            ((own_rows, fields * kk), F32),
            (extra_shape, F32),
        ],
        [
            VMEM((4, fields, 128), BF16),
            VMEM((fields, kk, examples), BF16),
            VMEM((units, examples), BF16),
            VMEM((quarter, examples), F32),
            VMEM((width, kk, examples), BF16),
            VMEM((width, kk, examples), F32),
            VMEM((3, part, kk, examples), BF16),
            VMEM((part, kk, examples), BF16),
            VMEM((part, kk, examples), BF16),
            VMEM((block, width, examples), F32),
            VMEM((4 * fields * slab, examples), F32),
            VMEM((nl * slab, examples), F32),
            VMEM((nl, part, examples), BF16),
        ]
        + row_scratch
        + [VMEM(cot_first.shape, BF16), VMEM((units, examples), BF16)]
        + row_scratch
        + [
            VMEM((nl // 2, part, examples), BF16),
            VMEM((nl // 2, part, examples), BF16),
            VMEM(cot_second.shape, BF16),
            VMEM(cot_second.shape, BF16),
            VMEM((16, 2, own_rows, columns), BF16),
            VMEM((16, 2, own_rows, fields * kk), BF16),
        ]
        + stages(columns)
        + stages(fields * kk)
        + [
            VMEM((fields, kk, examples), F32),
            VMEM((fields, slab, examples), F32),
            VMEM((width, kk, examples), BF16),
            VMEM((3, part, kk, examples), BF16),
            VMEM((part, kk, examples), BF16),
            VMEM((part, kk, examples), BF16),
            VMEM((width, examples), F32),
            VMEM(extra_shape, F32),
            VMEM((3,) + extra_shape, F32),
            VMEM(extra_shape, F32),
            VMEM(extra_shape, F32),
            pltpu.SemaphoreType.DMA((2, 7)),
            pltpu.SemaphoreType.DMA((2, 3)),
            pltpu.SemaphoreType.DMA((2, 3 * pieces)),
            pltpu.SemaphoreType.DMA((2, 7)),
            pltpu.SemaphoreType.DMA((2, 7)),
            pltpu.SemaphoreType.DMA((2, 12)),
            pltpu.SemaphoreType.DMA((2, 3)),
            pltpu.SemaphoreType.DMA((2, 4)),
            pltpu.SemaphoreType.DMA((2, 4)),
            pltpu.SemaphoreType.DMA((2, 7)),
            pltpu.SemaphoreType.DMA((2, 7)),
            pltpu.SemaphoreType.DMA((2, 4)),
        ],
        0,
        140,
        36,
        comp_part,
        w_linear,
        turned,
        w_up,
        up_bias.reshape(1, -1),
        w_down,
        cot_first,
        gain,
        cot_second,
    )
    spread = spread.reshape(4 * fields, part, examples)
    mixed = jnp.concatenate(
        [
            jnp.einsum("feb,neb->fn", spread, gathered, preferred_element_type=F32),
            jnp.einsum("feb,ekb->fk", spread, grad_comp, preferred_element_type=F32),
            jnp.zeros((4 * fields, 128 - nl - kk), F32),
        ],
        axis=1,
    ).reshape(4, fields, 128)
    total_rows = fields + 2 * n_extra
    grad_linear, grad_compress, extra = call(
        functools.partial(small_kernel, nl),
        [((fields, nl), F32), ((kk, fields), F32), (extra.shape, F32)],
        [
            VMEM((4, fields, 128), BF16),
            VMEM((3, fields, 128), BF16),
            VMEM((2, total_rows, 128), F32),
            VMEM((total_rows, 128), BF16),
            VMEM((3, total_rows, 128), BF16),
            VMEM((total_rows, 128), BF16),
            VMEM((3, total_rows, 128), BF16),
            pltpu.SemaphoreType.DMA((2, 10)),
        ],
        1,
        15,
        8,
        mixed,
        extra,
    )
    grad_bias = extra[:n_bias].reshape(-1)
    grad_gain = extra[n_bias, :width]
    return (
        fm_out.transpose(2, 0, 1),
        lc_out.transpose(2, 0, 1),
        grad_compress.T,
        grad_up,
        grad_bias,
        grad_down,
        grad_linear,
        grad_gain,
    )


def solution(mesh):
    placed = (
        P("batch", "field", None),
        P("field", None),
        P(None, "field"),
        P(),
        P(None, "field"),
        P("field", None),
        P(),
        P("batch", "field", None),
        P("batch", "field", None),
    )
    return jax.shard_map(
        local,
        mesh=mesh,
        in_specs=placed,
        out_specs=(
            P("batch", "field", None),
            P("batch", "field", None),
            P("field", None),
            P("batch", "field"),
            P(),
            P("batch", "field"),
            P("field", None),
            P(),
        ),
        check_vma=False,
    )
```

```python
import functools

import jax
import jax.numpy as jnp
from jax import lax
from jax.experimental import pallas as pl
from jax.experimental.pallas import tpu as pltpu
from jax.sharding import PartitionSpec as P

MESH = pl.DeviceIdType.MESH
VMEM = pltpu.VMEM
F32 = jnp.float32
BF16 = jnp.bfloat16
MIB = 1024 * 1024


class Place:
    def __init__(self):
        batch, field = lax.axis_index("batch"), lax.axis_index("field")
        self.batch, self.field = batch, field
        self.y, self.zh = lax.rem(field, 4), lax.div(field, 4)
        self.core = lax.rem(batch, 2)
        self.zl = lax.rem(lax.div(batch, 2), 4)
        self.x = lax.div(batch, 8)

    def to_y(self, k):
        other = lax.rem(self.y + k, 4)
        return other, (self.batch, self.zh * 4 + other)

    def to_zh(self):
        other = 1 - self.zh
        return other, (self.batch, other * 4 + self.y)

    def to_core(self):
        other = 1 - self.core
        return other, (self.x * 8 + self.zl * 2 + other, self.field)

    def to_x(self, k):
        other = lax.rem(self.x + k, 4)
        return other, (other * 8 + self.zl * 2 + self.core, self.field)

    def to_zl(self, k):
        other = lax.rem(self.zl + k, 4)
        return other, (self.x * 8 + other * 2 + self.core, self.field)

    def y_group(self):
        return [self.to_y(k)[1] for k in (1, 2, 3)]

    def field_group(self):
        return self.y_group() + [self.to_zh()[1]]

    def batch_group(self):
        return [self.to_core()[1]] + [self.to_x(k)[1] for k in (1, 2, 3)] + [self.to_zl(k)[1] for k in (1, 2, 3)]


def greet(peers, work=None):
    barrier = pltpu.get_barrier_semaphore()
    for peer in peers:
        pl.semaphore_signal(barrier, inc=1, device_id=peer, device_id_type=MESH)
    if work is not None:
        work()
    pl.semaphore_wait(barrier, len(peers))


def send(src, dst, sems, index, peer):
    copy = pltpu.make_async_remote_copy(
        src_ref=src,
        dst_ref=dst,
        send_sem=sems.at[0, index],
        recv_sem=sems.at[1, index],
        device_id=peer,
        device_id_type=MESH,
    )
    copy.start()
    return copy


def params(collective_id, mib):
    return pltpu.CompilerParams(
        collective_id=collective_id, has_side_effects=True, vmem_limit_bytes=mib * MIB
    )


def cost(us):
    return pl.CostEstimate(flops=0, bytes_accessed=int(us * 3.0e6), transcendentals=0)


def call(kernel, outs, scratch, collective_id, us, mib, *args):
    return pl.pallas_call(
        kernel,
        out_shape=[jax.ShapeDtypeStruct(shape, dtype) for shape, dtype in outs],
        in_specs=[pl.BlockSpec(memory_space=VMEM)] * len(args),
        out_specs=[pl.BlockSpec(memory_space=VMEM)] * len(outs),
        scratch_shapes=scratch,
        compiler_params=params(collective_id, mib),
        cost_estimate=cost(us),
    )(*args)


def rows(start, size):
    return pl.ds(pl.multiple_of(start * size, size), size)


def gather_rows(at, out_ref, sems):
    own = rows(at.y, out_ref.shape[0] // 4)
    return [send(out_ref.at[own], out_ref.at[own], sems, 3 + k, at.to_y(k)[1]) for k in (1, 2, 3)]


def mean0(values):
    return jnp.sum(values, axis=0, keepdims=True) * (1.0 / values.shape[0])


def norm(raw, cot, gain):
    centre = raw - mean0(raw)
    rstd = lax.rsqrt(mean0(centre * centre) + 1e-05)
    normed = centre * rstd
    dn = cot * gain
    grad = rstd * (dn - mean0(dn) - normed * mean0(dn * normed))
    return normed * gain, cot * normed, grad


class BatchSum:
    def __init__(self, at, ref, one, two, three, sems, out):
        self.at, self.ref, self.one, self.two, self.three, self.sems, self.out = (
            at, ref, one, two, three, sems, out,
        )

    def first(self):
        core, peer = self.at.to_core()
        self.copies = [send(self.ref.at[:, core], self.one, self.sems, 0, peer)]

    def wait(self):
        for copy in self.copies:
            copy.wait()

    def second(self):
        self.wait()
        one = self.one

        @pl.loop(0, 16)
        def _(j):
            one[j] = (one[j].astype(F32) + self.ref[j, self.at.core].astype(F32)).astype(BF16)

        self.copies = []
        for k in (1, 2, 3):
            x, peer = self.at.to_x(k)
            self.copies.append(send(one.at[pl.ds(x * 4, 4)], self.two.at[k - 1], self.sems, k, peer))

    def third(self):
        self.wait()
        for j in range(4):
            total = self.one[self.at.x * 4 + j].astype(F32)
            for k in range(3):
                total = total + self.two[k, j].astype(F32)
            self.two[0, j] = total.astype(BF16)
        self.copies = []
        for k in (1, 2, 3):
            z, peer = self.at.to_zl(k)
            self.copies.append(send(self.two.at[0, z], self.three.at[k - 1], self.sems, 3 + k, peer))

    def last(self):
        self.wait()
        total = self.two[0, self.at.zl].astype(F32)
        for k in range(3):
            total = total + self.three[k].astype(F32)
        self.out[...] = total


def layer_kernel(
    pieces,
    part_ref,
    wl_ref,
    emb_ref,
    up_ref,
    bias_ref,
    down_ref,
    cot_ref,
    gain_ref,
    lcot_ref,
    emb_out,
    fm_ref,
    out_ref,
    gather_ref,
    gcomp_ref,
    down_out,
    up_out,
    rows_out,
    wl_out,
    flat_ref,
    hidden_ref,
    pre_ref,
    comp,
    compf,
    ccgot,
    ccmine,
    ccother,
    embi,
    embx,
    linf,
    lin_ref,
    part,
    got,
    mine,
    other,
    gfm_ref,
    gpre_ref,
    hpart,
    hgot,
    hmine,
    hother,
    lmine,
    lother,
    raw_ref,
    glc,
    dpart,
    upart,
    d1,
    d2,
    d3,
    u1,
    u2,
    u3,
    interf,
    embf,
    cb,
    cgot,
    cmine,
    cother,
    rsum,
    rmine,
    rgot,
    rtotal,
    rother,
    ccsems,
    wsems,
    esems,
    psems,
    hsems,
    lsems,
    ysems,
    zsems,
    csems,
    dsems,
    usems,
    rsems,
):
    at = Place()
    fields, width, examples = emb_ref.shape
    step, kk = width // 4, part_ref.shape[1]
    scale = float(width) ** (-0.5)
    block = embi.shape[0]
    slab = embx.shape[0] // (4 * fields)
    background = []
    moved = []

    def piece(p):
        here = pl.ds(p % 2 * (fields // 2), fields // 2)
        for k in (1, 2, 3):
            y, peer = at.to_y(k)
            there = pl.ds(pl.multiple_of(y * step + p // 2 * slab, slab), slab)
            moved.append(
                send(
                    emb_ref.at[here, there, :],
                    emb_out.at[k, here, pl.ds(p // 2 * slab, slab), :],
                    esems,
                    p * 3 + k - 1,
                    peer,
                )
            )

    def own_part():
        wl_out[0] = jnp.zeros(wl_out.shape[1:], BF16)
        wl_out[0, :, : wl_ref.shape[1]] = wl_ref[...]
        emb_out[0] = emb_ref[:, rows(at.y, step), :]

    greet(at.field_group() + at.batch_group(), own_part)
    copies = []
    for k in (1, 2, 3):
        y, peer = at.to_y(k)
        copies.append(send(part_ref.at[rows(y, step)], ccgot.at[k - 1], ccsems, k - 1, peer))
    for k in (1, 2, 3):
        background.append(send(wl_out.at[0], wl_out.at[k], wsems, k - 1, at.to_y(k)[1]))
    for copy in copies:
        copy.wait()
    ccmine[...] = (
        part_ref[rows(at.y, step)].astype(F32)
        + ccgot[0].astype(F32)
        + ccgot[1].astype(F32)
        + ccgot[2].astype(F32)
    ).astype(BF16)
    copy = send(ccmine, ccother, ccsems, 3, at.to_zh()[1])
    piece(0)
    piece(1)
    copy.wait()
    own = rows(at.y, step)
    comp[own] = (ccmine[...].astype(F32) + ccother[...].astype(F32)).astype(BF16)
    copies = [send(comp.at[own], comp.at[own], ccsems, 3 + k, at.to_y(k)[1]) for k in (1, 2, 3)]
    for copy in copies:
        copy.wait()
    compf[...] = comp[...].astype(F32)

    def interact(start, stop):
        @pl.loop(start, stop)
        def _(i):
            embi[...] = emb_ref[pl.ds(i * block, block)].astype(F32)

            def terms(e, totals):
                c = compf[e]
                return tuple(t + c * embi[j, pl.ds(e, 1), :] for j, t in enumerate(totals))

            totals = lax.fori_loop(
                0, width, terms, tuple(jnp.zeros((kk, examples), F32) for _ in range(block)), unroll=8
            )
            for j in range(block):
                flat_ref[i * block + j] = (totals[j] * scale).astype(BF16)

    blocks = fields // block
    cuts = [blocks * p // 3 for p in range(4)]
    for p in range(3):
        if p < 2:
            piece(2 + p)
        interact(cuts[p], cuts[p + 1])

    flat = flat_ref[...].reshape(fields * kk, examples)
    units = up_ref.shape[0]
    quarter = units // 4

    @pl.loop(0, 4)
    def _(r):
        part[rows(r, quarter)] = jnp.dot(
            up_ref[rows(r, quarter), :], flat, preferred_element_type=F32
        ).astype(BF16)

    bias = jnp.transpose(jnp.broadcast_to(bias_ref[:, rows(at.y, quarter)], (examples, quarter)))
    copies = []
    for k in (1, 2, 3):
        y, peer = at.to_y(k)
        copies.append(send(part.at[rows(y, quarter)], got.at[k - 1], psems, k - 1, peer))

    for copy in background:
        copy.wait()
    wt = jnp.transpose(wl_out[...].reshape(4 * fields, wl_out.shape[2]).astype(F32))
    wt = wt[: lin_ref.shape[0]].astype(BF16)
    n_lin = lin_ref.shape[0]
    zh, zpeer = at.to_zh()
    lcopies = []

    def linear(g):
        for copy in moved[6 * g : 6 * g + 6]:
            copy.wait()
        for k in range(4):

            @pl.loop(0, fields // 8)
            def _(i):
                embx[rows(k * (fields // 8) + i, 8 * slab), :] = (
                    emb_out[k, pl.ds(i * 8, 8), g * slab : (g + 1) * slab, :]
                    .astype(F32)
                    .reshape(8 * slab, examples)
                )

        for e in range(slab):
            linf[pl.ds(e, n_lin, stride=slab), :] = jnp.dot(
                wt,
                embx[pl.ds(e, 4 * fields, stride=slab), :].astype(BF16),
                preferred_element_type=F32,
            )
        here = slice(g * slab, (g + 1) * slab)
        lin_ref[:, here, :] = linf[...].reshape(n_lin, slab, examples).astype(BF16)
        lcopies.append(
            send(
                lin_ref.at[pl.ds(zh * (n_lin // 2), n_lin // 2), here, :],
                lother.at[:, here, :],
                lsems,
                g,
                zpeer,
            )
        )

    linear(0)
    for copy in copies:
        copy.wait()
    mine[...] = (
        part[rows(at.y, quarter)].astype(F32)
        + got[0].astype(F32)
        + got[1].astype(F32)
        + got[2].astype(F32)
    ).astype(BF16)
    copy = send(mine, other, psems, 3, zpeer)
    piece(4)
    linear(1)
    copy.wait()
    pre = mine[...].astype(F32) + other[...].astype(F32) + bias
    pre_ref[...] = pre
    hidden_ref[rows(at.y, quarter)] = (pre / (1.0 + jnp.exp(-pre))).astype(BF16)
    for copy in gather_rows(at, hidden_ref, psems):
        copy.wait()
    chunk = raw_ref.shape[0]
    half = 4 * chunk
    zbase = at.zh * half
    own = rows(at.y, step)
    gain = gain_ref[...]
    ycopies = []

    def linear_sum(g):
        lcopies[g].wait()
        here = slice(g * slab, (g + 1) * slab)
        there = pl.ds(pl.multiple_of(at.y * step + g * slab, slab), slab)
        lmine[:, here, :] = (
            lin_ref[pl.ds(zbase, half), here, :].astype(F32) + lother[:, here, :].astype(F32)
        ).astype(BF16)
        for k in (1, 2, 3):
            y, peer = at.to_y(k)
            ycopies.append(
                send(
                    lmine.at[pl.ds(y * chunk, chunk), here, :],
                    raw_ref.at[:, there, :],
                    lsems,
                    3 + g * 3 + k - 1,
                    peer,
                )
            )
        raw_ref[:, there, :] = lmine[pl.ds(at.y * chunk, chunk), here, :]

    def column_sums(values):
        return jnp.sum(jnp.transpose(values), axis=0, keepdims=True)

    n_bias = units // rmine.shape[1]

    def forward():
        rmine[...] = jnp.zeros_like(rmine)
        hidden = jnp.transpose(hidden_ref[...].astype(F32)).astype(BF16)
        gain_total = jnp.zeros((width, examples), F32)
        for n in range(0, cot_ref.shape[0], 2):
            raw = jnp.transpose(
                jnp.dot(hidden, down_ref[:, n * width : (n + 2) * width], preferred_element_type=F32)
            )
            for m in range(2):
                out, term, grad = norm(
                    raw[m * width : (m + 1) * width], cot_ref[n + m].astype(F32), gain
                )
                fm_ref[n + m] = out.astype(BF16)
                gain_total = gain_total + term
                gfm_ref[n + m] = grad.astype(BF16)
        rsum[...] = gain_total

    piece(5)
    linear_sum(0)
    forward()
    gfm = gfm_ref[...].reshape(down_ref.shape[1], examples)

    @pl.loop(0, 4)
    def _(r):
        hpart[rows(r, quarter)] = jnp.dot(
            down_ref[rows(r, quarter), :], gfm, preferred_element_type=F32
        ).astype(BF16)

    copies = []
    for k in (1, 2, 3):
        y, peer = at.to_y(k)
        copies.append(send(hpart.at[rows(y, quarter)], hgot.at[k - 1], hsems, k - 1, peer))

    def weights(left_ref, right, into):
        @pl.loop(0, 4)
        def _(r):
            block = lax.dot_general(
                left_ref[rows(r, quarter), :],
                right,
                (((1,), (1,)), ((), ())),
                preferred_element_type=F32,
            ).astype(BF16)
            into[rows(r, 4)] = block.reshape((4,) + into.shape[1:])

    weights(hidden_ref, gfm, dpart)
    down = BatchSum(at, dpart, d1, d2, d3, dsems, down_out)
    down.first()
    linear_sum(1)
    for copy in copies:
        copy.wait()
    hmine[...] = (
        hpart[rows(at.y, quarter)].astype(F32)
        + hgot[0].astype(F32)
        + hgot[1].astype(F32)
        + hgot[2].astype(F32)
    ).astype(BF16)
    copy = send(hmine, hother, hsems, 3, zpeer)
    linear(2)
    down.second()
    pre = pre_ref[...]
    sigma = 1.0 / (1.0 + jnp.exp(-pre))
    slope = sigma * (1.0 + pre * (1.0 - sigma))
    copy.wait()
    grad = (hmine[...].astype(F32) + hother[...].astype(F32)) * slope
    gpre_ref[rows(at.y, quarter)] = grad.astype(BF16)
    copies = gather_rows(at, gpre_ref, hsems)
    rmine[pl.ds(at.y, 1), :] = 0.5 * column_sums(grad)
    linear_sum(2)
    for copy in copies:
        copy.wait()
    flat = flat_ref[...].reshape(fields * kk, examples)
    gpre = gpre_ref[...]
    @pl.loop(0, 6)
    def _(r):
        size = fields * kk // 6
        block = lax.dot_general(
            up_ref[:, rows(r, size)], gpre, (((0,), (0,)), ((), ())), preferred_element_type=F32
        ).astype(BF16)
        interf[rows(r, fields // 6)] = block.astype(F32).reshape(fields // 6, kk, examples)


    block = embf.shape[1]

    def compression(y):
        @pl.loop(0, step // block)
        def _(r):
            i = y * (step // block) + r
            embf[...] = emb_ref[:, rows(i, block), :].astype(F32)

            def terms(f, totals):
                g = interf[f]
                return tuple(t + g * embf[f, pl.ds(j, 1), :] for j, t in enumerate(totals))

            totals = lax.fori_loop(
                0, fields, terms, tuple(jnp.zeros((kk, examples), F32) for _ in range(block)), unroll=4
            )
            for j in range(block):
                cb[i * block + j] = totals[j].astype(BF16)

    for copy in ycopies:
        copy.wait()

    @pl.loop(0, chunk)
    def _(n):
        out, term, grad = norm(raw_ref[n].astype(F32), lcot_ref[n].astype(F32), gain)
        out_ref[n] = out.astype(BF16)
        rsum[...] += term
        glc[n] = grad.astype(BF16)

    mid = pl.ds(zbase + at.y * chunk, chunk)
    gather_ref[mid] = glc[:, own, :]
    zcopies = [send(gather_ref.at[mid], gather_ref.at[mid], zsems, 0, zpeer)]
    gcopies = []
    for k in (1, 2, 3):
        y, peer = at.to_y(k)
        gcopies.append(send(glc.at[:, rows(y, step), :], gather_ref.at[mid], ysems, k - 1, peer))
    rmine[n_bias : n_bias + 1, :width] = column_sums(rsum[...])
    rcopies = [send(rmine, rgot.at[k - 1], rsems, k - 1, at.to_y(k)[1]) for k in (1, 2, 3)]

    weights(gpre_ref, flat, upart)
    up = BatchSum(at, upart, u1, u2, u3, usems, up_out)
    up.first()
    down.third()
    ccopies = []

    def compression_to(k):
        y, peer = at.to_y(k)
        compression(y)
        ccopies.append(send(cb.at[rows(y, step)], cgot.at[k - 1], csems, k - 1, peer))

    compression_to(1)
    up.second()
    for k in (1, 2, 3):
        gcopies[k - 1].wait()
        source = lax.rem(at.y + 4 - k, 4)
        there = pl.ds(zbase + source * chunk, chunk)
        zcopies.append(send(gather_ref.at[there], gather_ref.at[there], zsems, k, zpeer))
    for copy in rcopies:
        copy.wait()
    rtotal[...] = (rmine[...] + rgot[1]) + (rgot[0] + rgot[2])
    rcopy = send(rtotal, rother, rsems, 3, zpeer)
    compression_to(2)
    compression_to(3)
    compression(at.y)
    up.third()
    for copy in ccopies:
        copy.wait()
    cmine[...] = (
        cb[own].astype(F32) + cgot[0].astype(F32) + cgot[1].astype(F32) + cgot[2].astype(F32)
    ).astype(BF16)
    ccopy = send(cmine, cother, csems, 3, zpeer)
    down.last()
    rcopy.wait()
    rows_out[...] = rtotal[...] + rother[...]
    ccopy.wait()
    gcomp_ref[...] = ((cmine[...].astype(F32) + cother[...].astype(F32)) * scale).astype(BF16)
    up.last()
    for copy in zcopies:
        copy.wait()


def small_kernel(
    nl, part_ref, rows_ref, lin_ref, comp_ref, rows_out, psend, ygot, one, xmine, xgot, zmine, zgot, sems
):
    at = Place()
    fields, kk = lin_ref.shape[0], comp_ref.shape[0]
    psend[...] = part_ref[...].astype(BF16)
    greet(at.y_group() + at.batch_group())
    copies = []
    for k in (1, 2, 3):
        copies.append(send(psend.at[k], ygot.at[k - 1], sems, k - 1, at.to_y(4 - k)[1]))
    half = rows_ref.shape[0]
    one[0, fields : fields + half] = rows_ref[:, :128]
    one[0, fields + half :] = rows_ref[:, 128:]
    for copy in copies:
        copy.wait()
    one[0, :fields] = (
        part_ref[0] + ygot[0].astype(F32) + ygot[1].astype(F32) + ygot[2].astype(F32)
    )
    send(one.at[0], one.at[1], sems, 3, at.to_core()[1]).wait()
    xmine[...] = (one[0] + one[1]).astype(BF16)
    copies = [send(xmine, xgot.at[k - 1], sems, 3 + k, at.to_x(k)[1]) for k in (1, 2, 3)]
    for copy in copies:
        copy.wait()
    zmine[...] = (
        (xmine[...].astype(F32) + xgot[1].astype(F32))
        + (xgot[0].astype(F32) + xgot[2].astype(F32))
    ).astype(BF16)
    copies = [send(zmine, zgot.at[k - 1], sems, 6 + k, at.to_zl(k)[1]) for k in (1, 2, 3)]
    for copy in copies:
        copy.wait()
    total = (zmine[...].astype(F32) + zgot[1].astype(F32)) + (
        zgot[0].astype(F32) + zgot[2].astype(F32)
    )
    lin_ref[...] = total[:fields, :nl]
    comp_ref[...] = jnp.transpose(total[:fields])[nl : nl + kk]
    rows_out[:, :128] = total[fields : fields + half]
    rows_out[:, 128:] = total[fields + half :]


def local(embeddings, compress, w_up, up_bias, w_down, w_linear, ln_gain, cot_fm, cot_lc):
    examples, fields, width = embeddings.shape
    units, kk, nl = w_up.shape[0], compress.shape[1], w_linear.shape[1]
    part, quarter, own_rows = width // 4, units // 4, units // 32
    turned = embeddings.transpose(1, 2, 0)
    gain = jnp.broadcast_to(ln_gain.reshape(-1, 1), (width, examples))
    comp_part = jnp.einsum("feb,fk->ekb", turned, compress, preferred_element_type=F32).astype(BF16)
    cot_first, cot_second = cot_fm.transpose(1, 2, 0), cot_lc.transpose(1, 2, 0)
    pieces, block = 6, 8

    def stages(columns):
        return [
            VMEM((16, own_rows, columns), BF16),
            VMEM((3, 4, own_rows, columns), BF16),
            VMEM((3, own_rows, columns), BF16),
        ]

    row_scratch = [
        VMEM((units, examples), BF16),
        VMEM((3, quarter, examples), BF16),
        VMEM((quarter, examples), BF16),
        VMEM((quarter, examples), BF16),
    ]
    columns = cot_first.shape[0] * width
    extra_shape = (8, 256)
    n_bias, n_extra, slab = units // 256, 8, 16
    spread, fm_out, lc_out, gathered, grad_comp, grad_down, grad_up, extra = call(
        functools.partial(layer_kernel, pieces),
        [
            ((4, fields, part, examples), BF16),
            (cot_first.shape, BF16),
            (cot_second.shape, BF16),
            ((nl, part, examples), BF16),
            ((part, kk, examples), BF16),
            ((own_rows, columns), F32),
            ((own_rows, fields * kk), F32),
            (extra_shape, F32),
        ],
        [
            VMEM((4, fields, 128), BF16),
            VMEM((fields, kk, examples), BF16),
            VMEM((units, examples), BF16),
            VMEM((quarter, examples), F32),
            VMEM((width, kk, examples), BF16),
            VMEM((width, kk, examples), F32),
            VMEM((3, part, kk, examples), BF16),
            VMEM((part, kk, examples), BF16),
            VMEM((part, kk, examples), BF16),
            VMEM((block, width, examples), F32),
            VMEM((4 * fields * slab, examples), F32),
            VMEM((nl * slab, examples), F32),
            VMEM((nl, part, examples), BF16),
        ]
        + row_scratch
        + [VMEM(cot_first.shape, BF16), VMEM((units, examples), BF16)]
        + row_scratch
        + [
            VMEM((nl // 2, part, examples), BF16),
            VMEM((nl // 2, part, examples), BF16),
            VMEM(cot_second.shape, BF16),
            VMEM(cot_second.shape, BF16),
            VMEM((16, 2, own_rows, columns), BF16),
            VMEM((16, 2, own_rows, fields * kk), BF16),
        ]
        + stages(columns)
        + stages(fields * kk)
        + [
            VMEM((fields, kk, examples), F32),
            VMEM((fields, slab, examples), F32),
            VMEM((width, kk, examples), BF16),
            VMEM((3, part, kk, examples), BF16),
            VMEM((part, kk, examples), BF16),
            VMEM((part, kk, examples), BF16),
            VMEM((width, examples), F32),
            VMEM(extra_shape, F32),
            VMEM((3,) + extra_shape, F32),
            VMEM(extra_shape, F32),
            VMEM(extra_shape, F32),
            pltpu.SemaphoreType.DMA((2, 7)),
            pltpu.SemaphoreType.DMA((2, 3)),
            pltpu.SemaphoreType.DMA((2, 3 * pieces)),
            pltpu.SemaphoreType.DMA((2, 7)),
            pltpu.SemaphoreType.DMA((2, 7)),
            pltpu.SemaphoreType.DMA((2, 12)),
            pltpu.SemaphoreType.DMA((2, 3)),
            pltpu.SemaphoreType.DMA((2, 4)),
            pltpu.SemaphoreType.DMA((2, 4)),
            pltpu.SemaphoreType.DMA((2, 7)),
            pltpu.SemaphoreType.DMA((2, 7)),
            pltpu.SemaphoreType.DMA((2, 4)),
        ],
        0,
        140,
        36,
        comp_part,
        w_linear,
        turned,
        w_up,
        up_bias.reshape(1, -1),
        w_down,
        cot_first,
        gain,
        cot_second,
    )
    spread = spread.reshape(4 * fields, part, examples)
    mixed = jnp.concatenate(
        [
            jnp.einsum("feb,neb->fn", spread, gathered, preferred_element_type=F32),
            jnp.einsum("feb,ekb->fk", spread, grad_comp, preferred_element_type=F32),
            jnp.zeros((4 * fields, 128 - nl - kk), F32),
        ],
        axis=1,
    ).reshape(4, fields, 128)
    total_rows = fields + 2 * n_extra
    grad_linear, grad_compress, extra = call(
        functools.partial(small_kernel, nl),
        [((fields, nl), F32), ((kk, fields), F32), (extra.shape, F32)],
        [
            VMEM((4, fields, 128), BF16),
            VMEM((3, fields, 128), BF16),
            VMEM((2, total_rows, 128), F32),
            VMEM((total_rows, 128), BF16),
            VMEM((3, total_rows, 128), BF16),
            VMEM((total_rows, 128), BF16),
            VMEM((3, total_rows, 128), BF16),
            pltpu.SemaphoreType.DMA((2, 10)),
        ],
        1,
        15,
        8,
        mixed,
        extra,
    )
    grad_bias = extra[:n_bias].reshape(-1)
    grad_gain = extra[n_bias, :width]
    return (
        fm_out.transpose(2, 0, 1),
        lc_out.transpose(2, 0, 1),
        grad_compress.T,
        grad_up,
        grad_bias,
        grad_down,
        grad_linear,
        grad_gain,
    )


def solution(mesh):
    placed = (
        P("batch", "field", None),
        P("field", None),
        P(None, "field"),
        P(),
        P(None, "field"),
        P("field", None),
        P(),
        P("batch", "field", None),
        P("batch", "field", None),
    )
    return jax.shard_map(
        local,
        mesh=mesh,
        in_specs=placed,
        out_specs=(
            P("batch", "field", None),
            P("batch", "field", None),
            P("field", None),
            P("batch", "field"),
            P(),
            P("batch", "field"),
            P("field", None),
            P(),
        ),
        check_vma=False,
    )
```
